32 devices in a mesh: stream: 2 (over x), dp: 16 (over z, y, core).
Axes of the slice: x: 2, y: 2, z: 4, core: 2. Of those that a mesh axis runs over, the one named last changes fastest.
Arguments:
- hidden: bfloat16 [2, 384, 36, 768], P('stream', 'dp'), may hold values from -6 to 6
- lengths: int32 [2, 384], P('stream', 'dp'), may hold values from 4 to 36, as said below
- task_flags: int32 [2, 384], P('stream', 'dp'), may hold values 0 or 1
- cotangent: bfloat16 [2, 384, 36, 768], P('stream', 'dp'), may hold values from -6 to 6
- cross_proj: bfloat16 [768, 2304], replicated, may hold values from -0.21875 to 0.21875
- cross_bias: float32 [3, 768], replicated, may hold values from -3 to 3
- cross_norm: float32 [2, 768], replicated, may hold values from 0.25 to 1.75
- cross_out: bfloat16 [768, 768], replicated, may hold values from -0.875 to 0.875
- self_proj: bfloat16 [2, 768, 2304], P('stream'), may hold values from -0.21875 to 0.21875
- self_bias: float32 [2, 3, 768], P('stream'), may hold values from -3 to 3
- self_norm: float32 [2, 2, 768], P('stream'), may hold values from 0.25 to 1.75
- self_out: bfloat16 [2, 768, 768], P('stream'), may hold values from -0.875 to 0.875
- ffn_up: bfloat16 [2, 768, 3072], P('stream'), may hold values from -0.21875 to 0.21875
- up_bias: float32 [2, 3072], P('stream'), may hold values from -3 to 3
- ffn_down: bfloat16 [2, 3072, 768], P('stream'), may hold values from -0.109375 to 0.109375
- down_bias: float32 [2, 768], P('stream'), may hold values from -3 to 3
- ffn_norm: float32 [2, 2, 768], P('stream'), may hold values from 0.25 to 1.75
Outputs:
- output: bfloat16 [2, 384, 36, 768], P('stream', 'dp')
- grad_hidden: bfloat16 [2, 384, 36, 768], P('stream', 'dp')
- grad_cross_proj: float32 [768, 2304], P(('stream', 'dp'))
- grad_cross_bias: float32 [3, 768], P(None, ('stream', 'dp'))
- grad_cross_norm: float32 [2, 768], P(None, ('stream', 'dp'))
- grad_cross_out: float32 [768, 768], P(('stream', 'dp'))
- grad_self_proj: float32 [2, 768, 2304], P('stream', 'dp')
- grad_self_bias: float32 [2, 3, 768], P('stream', None, 'dp')
- grad_self_norm: float32 [2, 2, 768], P('stream', None, 'dp')
- grad_self_out: float32 [2, 768, 768], P('stream', 'dp')
- grad_ffn_up: float32 [2, 768, 3072], P('stream', 'dp')
- grad_up_bias: float32 [2, 3072], P('stream', 'dp')
- grad_ffn_down: float32 [2, 3072, 768], P('stream', 'dp')
- grad_down_bias: float32 [2, 768], P('stream', 'dp')
- grad_ffn_norm: float32 [2, 2, 768], P('stream', None, 'dp')
The draws below stay inside these ranges and needn't reach their ends.
Inputs may be any that keep to these rules, and one draw needn't show every extreme that they name: `lengths`: stream 0 (words) has 4 to 20 live slots an item and some item has exactly 20; stream 1 (regions) has 12 to 36 and some item has exactly 36.
All inputs are finite; a program needn't handle non-finite values. No bound on the sum of `task_flags` on one device may be relied on, other than what follows from the above.
Results may differ from the reference program's by a relative error of at most 0.02.
Values may be sent and summed in bfloat16 or wider, within the bound.
A program may use at most 192 MiB of HBM per device.

```python
import jax
import jax.numpy as jnp
from jax import lax

D = 768
HEADS = 12
HEAD_DIM = 64
FF = 3072
WORDS = 20
REGIONS = 36
LEN = 36
ITEMS = 384


def draw_lengths(key, part):
    key = jax.random.fold_in(key, 7)
    first_key, second_key, third_key = jax.random.split(key, 3)
    word_counts = jax.random.randint(first_key, (ITEMS,), 4, WORDS + 1)
    region_counts = jax.random.randint(second_key, (ITEMS,), REGIONS // 3, REGIONS + 1)
    chosen = jax.random.randint(third_key, (2,), 0, ITEMS)
    indices = jnp.arange(ITEMS)
    word_counts = jnp.where(indices == chosen[0], WORDS, word_counts)
    region_counts = jnp.where(indices == chosen[1], REGIONS, region_counts)
    return jnp.stack([word_counts, region_counts]).astype(jnp.int32)


def place_ends(entries, stream_key, least, high):
    shape = entries.shape
    spot = [jax.random.randint(jax.random.fold_in(stream_key, axis), (), 0, shape[axis]) for axis in range(len(shape))]
    entries = entries.at[tuple(spot)].set(least)
    longest = shape.index(max(shape))
    spot[longest] = (spot[longest] + 1) % shape[longest]
    return entries.at[tuple(spot)].set(high)


def levels(rng, shape, shards, least, top_value):
    loudness, own = 1.0, jax.random.fold_in(rng, 6)
    for axis_at, parts in shards:
        steps = jnp.exp(jax.random.uniform(jax.random.fold_in(own, axis_at), (parts,), jnp.float32, least / len(shards), top_value / len(shards)))
        loudness = loudness * jnp.repeat(steps, shape[axis_at] // parts).reshape([-1 if axis == axis_at else 1 for axis in range(len(shape))])
    return loudness


def normal_values(key, shape, scale, limit, cuts=(), kind=jnp.bfloat16):
    values = jax.random.normal(key, shape, jnp.float32) * scale
    if len(cuts) > 0:
        values = levels(key, shape, cuts, -0.22, 0.18) * values
    return jnp.clip(values, min=-limit, max=limit).astype(kind)


def setup_inputs(seed: int = 0) -> dict:
    splits = jax.random.split(jax.random.key(seed), 18)
    hidden = normal_values(splits[0], (2, ITEMS, LEN, D), 1.0, 6.0, ((0, 2), (1, 16)))
    lengths = draw_lengths(jax.random.fold_in(splits[17], 71), 0)
    task_flags = place_ends((jax.random.randint(splits[2], (2, ITEMS), 0, 4) < 3).astype(jnp.int32), jax.random.fold_in(splits[2], 1), 0, 1)
    cotangent = normal_values(splits[3], (2, ITEMS, LEN, D), 1.0, 6.0, ((0, 2), (1, 16)))
    cross_proj = normal_values(splits[4], (D, 3 * D), D ** -0.5, 0.21875)
    cross_bias = normal_values(splits[5], (3, D), 0.3, 3.0, (), jnp.float32)
    cross_norm = jnp.clip(1.0 + 0.15 * jax.random.normal(splits[6], (2, D), jnp.float32), 0.25, 1.75)
    cross_out = normal_values(splits[7], (D, D), (D // 16) ** -0.5, 0.875)
    self_proj = normal_values(splits[8], (2, D, 3 * D), D ** -0.5, 0.21875, ((0, 2),))
    self_bias = normal_values(splits[9], (2, 3, D), 0.3, 3.0, ((0, 2),), jnp.float32)
    self_norm = jnp.clip(1.0 + 0.15 * jax.random.normal(splits[10], (2, 2, D), jnp.float32), 0.25, 1.75)
    self_out = normal_values(splits[11], (2, D, D), (D // 16) ** -0.5, 0.875, ((0, 2),))
    ffn_up = normal_values(splits[12], (2, D, FF), D ** -0.5, 0.21875, ((0, 2),))
    up_bias = normal_values(splits[13], (2, FF), 0.3, 3.0, ((0, 2),), jnp.float32)
    ffn_down = normal_values(splits[14], (2, FF, D), FF ** -0.5, 0.109375, ((0, 2),))
    down_bias = normal_values(splits[15], (2, D), 0.3, 3.0, ((0, 2),), jnp.float32)
    ffn_norm = jnp.clip(1.0 + 0.15 * jax.random.normal(splits[16], (2, 2, D), jnp.float32), 0.25, 1.75)
    return dict(hidden=hidden, lengths=lengths, task_flags=task_flags, cotangent=cotangent, cross_proj=cross_proj, cross_bias=cross_bias, cross_norm=cross_norm, cross_out=cross_out, self_proj=self_proj, self_bias=self_bias, self_norm=self_norm, self_out=self_out, ffn_up=ffn_up, up_bias=up_bias, ffn_down=ffn_down, down_bias=down_bias, ffn_norm=ffn_norm)


@jax.custom_vjp
def low(v):
    return lax.optimization_barrier(v.astype(jnp.bfloat16)).astype(jnp.float32)

@jax.custom_vjp
def low_back(v):
    return v

def low_keep(v):
    return (low(v), None)

def low_pass(kept, grad):
    return (grad,)

def back_keep(v):
    return (v, None)

def back_low(kept, grad):
    return (low(grad),)
low.defvjp(low_keep, low_pass)
low_back.defvjp(back_keep, back_low)
norm_eps = 1e-06
item_block = 32

def matmul(left_side, right_side):
    return jnp.dot(left_side, right_side, precision=lax.Precision.HIGHEST)

def layer_norm(summed, norm_gain, norm_shift):
    centred = summed - lax.optimization_barrier(jnp.mean(summed, axis=-1, keepdims=True))
    spread = lax.optimization_barrier(jnp.mean(centred * centred, axis=-1, keepdims=True))
    return centred * lax.rsqrt(spread + norm_eps) * norm_gain + norm_shift

def split_heads(tensor):
    return tensor.reshape(tensor.shape[0], LEN, HEADS, HEAD_DIM)

def attend(queries, key_rows, value_rows, key_len):
    scores = jnp.einsum('bqhd,bkhd->bhqk', split_heads(queries), split_heads(key_rows), precision=lax.Precision.HIGHEST) * HEAD_DIM ** (-0.5)
    scores = low_back(scores)
    allowed = (jnp.arange(LEN)[None, :] < key_len[:, None])[:, None, None, :]
    scores = jnp.where(allowed, scores, -1000000000.0)
    weights = jax.nn.softmax(scores, axis=-1)
    context = jnp.einsum('bhqk,bkhd->bqhd', low(weights), split_heads(value_rows), precision=lax.Precision.HIGHEST)
    return context.reshape(context.shape[0], LEN, D)

def forward(params, inputs, lengths):
    cross_proj, cross_bias, cross_norm, cross_out, self_proj, self_bias, self_norm, self_out, ffn_up, up_bias, ffn_down, down_bias, ffn_norm = params
    zero_row = jnp.zeros((D,), jnp.float32)
    rounded = [low(inputs[0]), low(inputs[1])]
    queries = []
    key_rows = []
    value_rows = []
    for stream in range(2):
        queries.append(low(low_back(matmul(rounded[stream], cross_proj[:, :D]) + cross_bias[0])))
        paired = low(low_back(matmul(rounded[stream], cross_proj[:, D:]) + jnp.concatenate([zero_row, cross_bias[1]])))
        key_rows.append(paired[..., :D])
        value_rows.append(paired[..., D:])
    results = []
    for stream in range(2):
        partner = 1 - stream
        context = low(low_back(attend(queries[stream], key_rows[partner], value_rows[partner], lengths[partner])))
        summed = low_back(matmul(context, cross_out) + cross_bias[2]) + inputs[stream]
        crossed = layer_norm(summed, cross_norm[0], cross_norm[1])
        triple = matmul(low(crossed), self_proj[stream]) + jnp.concatenate([self_bias[stream, 0], zero_row, self_bias[stream, 1]])
        triple = low(low_back(triple))
        context = low(low_back(attend(triple[..., :D], triple[..., D:2 * D], triple[..., 2 * D:], lengths[stream])))
        summed = low_back(matmul(context, self_out[stream]) + self_bias[stream, 2]) + crossed
        attended = layer_norm(summed, self_norm[stream, 0], self_norm[stream, 1])
        expanded = low_back(matmul(low(attended), ffn_up[stream]) + up_bias[stream])
        activated = low(jax.nn.gelu(expanded, approximate=False))
        summed = low_back(matmul(activated, ffn_down[stream]) + down_bias[stream]) + attended
        results.append(layer_norm(summed, ffn_norm[stream, 0], ffn_norm[stream, 1]))
    return jnp.stack(results)

def add_all(earlier, later):
    return earlier + later

def reference(hidden, lengths, task_flags, cotangent, cross_proj, cross_bias, cross_norm, cross_out, self_proj, self_bias, self_norm, self_out, ffn_up, up_bias, ffn_down, down_bias, ffn_norm):
    params = tuple((weight.astype(jnp.float32) for weight in (cross_proj, cross_bias, cross_norm, cross_out, self_proj, self_bias, self_norm, self_out, ffn_up, up_bias, ffn_down, down_bias, ffn_norm)))
    blocks = ITEMS // item_block

    def regroup(tensor):
        return jnp.moveaxis(tensor.reshape((2, blocks, item_block) + tensor.shape[2:]), 1, 0)
    positions = jnp.arange(LEN)

    def block_step(totals, pieces):
        inputs, cot_block, len_block, flag_block = pieces
        live_rows = (positions[None, None, :] < len_block[:, :, None]) & (flag_block[:, :, None] > 0)
        result, pullback = jax.vjp(lambda weights, activations: forward(weights, activations, len_block), params, inputs)
        grad_params, grad_inputs = pullback(cot_block * live_rows[..., None].astype(jnp.float32))
        totals = jax.tree.map(add_all, totals, grad_params)
        return (totals, (result, grad_inputs))
    zero_grads = jax.tree.map(jnp.zeros_like, params)
    totals, (outputs, input_grads) = lax.scan(block_step, zero_grads, (regroup(hidden.astype(jnp.float32)), regroup(cotangent.astype(jnp.float32)), regroup(lengths), regroup(task_flags)))

    def ungroup(tensor):
        return jnp.moveaxis(tensor, 0, 1).reshape((2, ITEMS, LEN, D))
    return (ungroup(outputs).astype(jnp.bfloat16), ungroup(input_grads).astype(jnp.bfloat16), totals[0], totals[1], totals[2], totals[3], totals[4], totals[5], totals[6], totals[7], totals[8], totals[9], totals[10], totals[11], totals[12])
```

```python
import functools

import jax
import jax.numpy as jnp
from jax import lax
from jax.experimental import pallas as pl
from jax.experimental.pallas import tpu as pltpu
from jax.sharding import PartitionSpec as P

HEADS = 12
HEAD_DIM = 64
PAIRS = HEADS // 2
LANES = 2 * HEAD_DIM

norm_eps = 1e-06
masked_score = -1000000000.0
vmem_limit = 60 * 1024 * 1024

f32 = jnp.float32
bf16 = jnp.bfloat16


def dot(left, right):
    return jnp.dot(left, right, preferred_element_type=f32)


def dot_nt(left, right):
    return lax.dot_general(left, right, (((1,), (1,)), ((), ())), preferred_element_type=f32)


def dot_tn(left, right):
    return lax.dot_general(left, right, (((0,), (0,)), ((), ())), preferred_element_type=f32)


def norm_parts(summed):
    centred = summed - jnp.mean(summed, axis=-1, keepdims=True)
    scaled = lax.rsqrt(jnp.mean(centred * centred, axis=-1, keepdims=True) + norm_eps)
    return centred * scaled, scaled


def norm_backward(upstream, normed, scaled, gain):
    inner = upstream * gain
    return scaled * (
        inner
        - jnp.mean(inner, axis=-1, keepdims=True)
        - normed * jnp.mean(inner * normed, axis=-1, keepdims=True)
    )


def row_sum(rows):
    return jnp.sum(rows, axis=0, keepdims=True)


def gelu_parts(entries):
    size = jnp.abs(entries)
    bell = jnp.exp(entries * entries * -0.5)
    t = 1.0 / (1.0 + size * (0.3275911 * 0.7071067811865476))
    poly = t * (
        0.5 * 0.254829592
        + t
        * (
            0.5 * -0.284496736
            + t * (0.5 * 1.421413741 + t * (0.5 * -1.453152027 + t * (0.5 * 1.061405429)))
        )
    )
    tail = poly * bell
    area = jnp.where(entries >= 0.0, 1.0 - tail, tail)
    return entries * area, area + entries * bell * 0.3989422804014327


def densify(dense_ref, block_ref, items, slots):
    for item in range(items):
        dense_ref[item * slots : (item + 1) * slots, :] = block_ref[0, item].astype(f32)


def pair_mask(len_ref, first, slots):
    shape = (2 * slots, 2 * slots)
    row = lax.broadcasted_iota(jnp.int32, shape, 0)
    col = lax.broadcasted_iota(jnp.int32, shape, 1)
    far_row = row >= slots
    low = jnp.where(far_row, slots, 0)
    high = jnp.where(far_row, slots + len_ref[0, first + 1], len_ref[0, first])
    allowed = (col >= low) & (col < high)
    return jnp.concatenate([allowed, allowed], axis=0)


def head_stack(rows):
    lane = lax.broadcasted_iota(jnp.int32, rows.shape, 1)
    return jnp.concatenate(
        [jnp.where(lane < HEAD_DIM, rows, 0.0), jnp.where(lane < HEAD_DIM, 0.0, rows)], axis=0
    ).astype(bf16)


def head_merge(stacked):
    count = stacked.shape[0] // 2
    lane = lax.broadcasted_iota(jnp.int32, (count, stacked.shape[1]), 1)
    return jnp.where(lane < HEAD_DIM, stacked[:count], stacked[count:])


def attend(triple_ref, context_ref, probs_ref, len_ref, first_item, items, slots):
    span = 2 * slots
    width = HEADS * HEAD_DIM

    def unit(u, carry):
        rows = pl.ds(pl.multiple_of(u * 2 * span, 2 * span), 2 * span)
        masks = [pair_mask(len_ref, first_item + 4 * u + 2 * g, slots) for g in range(2)]
        for pair in range(PAIRS):
            at = pair * LANES
            queries = triple_ref[rows, at : at + LANES].astype(f32) * HEAD_DIM**-0.5
            keys = triple_ref[rows, width + at : width + at + LANES].astype(f32)
            values = triple_ref[rows, 2 * width + at : 2 * width + at + LANES].astype(f32)
            merged = []
            for g in range(2):
                part = slice(g * span, (g + 1) * span)
                scores = dot_nt(head_stack(queries[part]), keys[part].astype(bf16))
                scores = jnp.where(masks[g], scores, masked_score)
                exponent = jnp.exp(scores - jnp.max(scores, axis=-1, keepdims=True))
                probs = exponent * (1.0 / jnp.sum(exponent, axis=-1, keepdims=True))
                probs = probs.astype(bf16)
                probs_ref[2 * u + g, pair] = probs
                merged.append(head_merge(dot(probs, values[part].astype(bf16))))
            context_ref[rows, at : at + LANES] = jnp.concatenate(merged, axis=0).astype(bf16)
        return carry

    lax.fori_loop(0, items // 4, unit, 0)


def attend_back(triple_ref, probs_ref, grad_ref, grad_triple_ref, row_base, items, slots):
    span = 2 * slots
    width = HEADS * HEAD_DIM

    def unit(u, carry):
        rows = pl.ds(pl.multiple_of(u * 2 * span, 2 * span), 2 * span)
        out_rows = pl.ds(pl.multiple_of(row_base + u * 2 * span, 2 * span), 2 * span)
        for pair in range(PAIRS):
            at = pair * LANES
            queries = triple_ref[rows, at : at + LANES].astype(f32) * HEAD_DIM**-0.5
            keys = triple_ref[rows, width + at : width + at + LANES].astype(f32)
            values = triple_ref[rows, 2 * width + at : 2 * width + at + LANES].astype(f32)
            grads = grad_ref[rows, at : at + LANES].astype(f32)
            merged = [[], [], []]
            for g in range(2):
                part = slice(g * span, (g + 1) * span)
                key_low = keys[part].astype(bf16)
                query_stack = head_stack(queries[part])
                grad_stack = head_stack(grads[part])
                probs = probs_ref[2 * u + g, pair]
                wide = probs.astype(f32)
                grad_probs = dot_nt(grad_stack, values[part].astype(bf16))
                product = wide * grad_probs
                grad_scores = product - wide * jnp.sum(product, axis=-1, keepdims=True)
                grad_scores = grad_scores.astype(bf16)
                merged[0].append(head_merge(dot(grad_scores, key_low)) * HEAD_DIM**-0.5)
                merged[1].append(dot_tn(grad_scores, query_stack))
                merged[2].append(dot_tn(probs, grad_stack))
            for part in range(3):
                grad_triple_ref[out_rows, part * width + at : part * width + at + LANES] = (
                    jnp.concatenate(merged[part], axis=0).astype(bf16)
                )
        return carry

    lax.fori_loop(0, items // 4, unit, 0)


def forward_kernel(
    items, slots,
    far_len, own_len, hidden, far, cross_proj, cross_bias, cross_norm, cross_out, self_proj, self_bias, self_norm, self_out,
    dense, far_dense, triple1, probs1, context1, normed1, scale1, triple2, probs2, context2, normed2, scale2,
    wide, far_wide,
):
    width = HEADS * HEAD_DIM
    first = pl.program_id(0) * items
    densify(wide, hidden, items, slots)
    densify(far_wide, far, items, slots)
    low = wide[...].astype(bf16)
    dense[...] = low
    far_low = far_wide[...].astype(bf16)
    far_dense[...] = far_low
    triple1[:, :width] = (dot(low, cross_proj[:, :width]) + cross_bias[0:1]).astype(bf16)
    triple1[:, width : 2 * width] = dot(far_low, cross_proj[:, width : 2 * width]).astype(bf16)
    triple1[:, 2 * width :] = (dot(far_low, cross_proj[:, 2 * width :]) + cross_bias[1:2]).astype(bf16)
    attend(triple1, context1, probs1, far_len, first, items, slots)
    normed, scale = norm_parts(dot(context1[...], cross_out[...]) + cross_bias[2:3] + wide[...])
    normed1[...] = normed
    scale1[...] = scale
    crossed = normed * cross_norm[0:1] + cross_norm[1:2]
    wide[...] = crossed
    low = crossed.astype(bf16)
    triple2[:, :width] = (dot(low, self_proj[0, :, :width]) + self_bias[0, 0:1]).astype(bf16)
    triple2[:, width : 2 * width] = dot(low, self_proj[0, :, width : 2 * width]).astype(bf16)
    triple2[:, 2 * width :] = (dot(low, self_proj[0, :, 2 * width :]) + self_bias[0, 1:2]).astype(bf16)
    attend(triple2, context2, probs2, own_len, first, items, slots)
    normed, scale = norm_parts(dot(context2[...], self_out[0]) + self_bias[0, 2:3] + wide[...])
    normed2[...] = normed
    scale2[...] = scale


def ffn_kernel(
    items, slots,
    own_len, flags, normed2, cotangent, self_norm, ffn_up, up_bias, ffn_down, down_bias, ffn_norm,
    output, grad_attended, attended_low, activated, grad_last_low, grad_expanded, up_sum, vec_sum,
    slope, wide,
):
    width = HEADS * HEAD_DIM
    chunks = ffn_up.shape[2] // width
    step = pl.program_id(0)
    first = step * items

    @pl.when(step == 0)
    def _():
        up_sum[...] = jnp.zeros_like(up_sum)
        vec_sum[...] = jnp.zeros_like(vec_sum)

    attended = normed2[...] * self_norm[0, 0:1] + self_norm[0, 1:2]
    low = attended.astype(bf16)
    attended_low[...] = low
    total = attended + down_bias[...]
    for chunk in range(chunks):
        at = slice(chunk * width, (chunk + 1) * width)
        active, rise = gelu_parts(dot(low, ffn_up[0, :, at]) + up_bias[:, at])
        active = active.astype(bf16)
        activated[:, at] = active
        slope[:, at] = rise
        total = total + dot(active, ffn_down[0, at, :])
    normed, scale = norm_parts(total)
    wide[...] = normed * ffn_norm[0, 0:1] + ffn_norm[0, 1:2]
    for item in range(items):
        output[0, item] = wide[item * slots : (item + 1) * slots, :].astype(bf16)
    slot = lax.broadcasted_iota(jnp.int32, (slots, width), 0)
    for item in range(items):
        live = jnp.where(flags[0, first + item] > 0, own_len[0, first + item], 0)
        wide[item * slots : (item + 1) * slots, :] = jnp.where(
            slot < live, cotangent[0, item].astype(f32), 0.0
        )
    upstream = wide[...]
    grad_last = norm_backward(upstream, normed, scale, ffn_norm[0, 0:1])
    grad_low = grad_last.astype(bf16)
    grad_last_low[...] = grad_low
    vec_sum[0:1] += row_sum(grad_low.astype(f32))
    vec_sum[1:2] += row_sum(upstream * normed)
    vec_sum[2:3] += row_sum(upstream)
    total = grad_last
    for chunk in range(chunks):
        at = slice(chunk * width, (chunk + 1) * width)
        grad_up = (dot_nt(grad_low, ffn_down[0, at, :]) * slope[:, at]).astype(bf16)
        grad_expanded[:, at] = grad_up
        up_sum[:, at] += row_sum(grad_up.astype(f32))
        total = total + dot_nt(grad_up, ffn_up[0, :, at])
    grad_attended[...] = total


def self_back_kernel(
    items, slots,
    grad_attended, normed2, scale2, normed1, triple2, probs2, cross_norm, self_norm, self_proj, self_out,
    grad_crossed, crossed_low, grad_mid_low, grad_triple, vec_sum,
    grad_context,
):
    width = HEADS * HEAD_DIM

    @pl.when(pl.program_id(0) == 0)
    def _():
        vec_sum[...] = jnp.zeros_like(vec_sum)

    upstream = grad_attended[...]
    normed = normed2[...]
    grad_mid = norm_backward(upstream, normed, scale2[...], self_norm[0, 0:1])
    low = grad_mid.astype(bf16)
    grad_mid_low[...] = low
    vec_sum[2:3] += row_sum(low.astype(f32))
    vec_sum[3:4] += row_sum(upstream * normed)
    vec_sum[4:5] += row_sum(upstream)
    grad_context[...] = dot_nt(low, self_out[0]).astype(bf16)
    attend_back(triple2, probs2, grad_context, grad_triple, 0, items, slots)
    vec_sum[0:1] += row_sum(grad_triple[:, :width].astype(f32))
    vec_sum[1:2] += row_sum(grad_triple[:, 2 * width :].astype(f32))
    crossed_low[...] = (normed1[...] * cross_norm[0:1] + cross_norm[1:2]).astype(bf16)
    grad_crossed[...] = grad_mid + dot_nt(grad_triple[...], self_proj[0])


def cross_back_kernel(
    items, slots,
    grad_crossed, normed1, scale1, triple1, probs1, cross_norm, cross_proj, cross_out,
    grad_own, grad_far, grad_cross_low, grad_triple, vec_sum,
    grad_context,
):
    width = HEADS * HEAD_DIM

    @pl.when(pl.program_id(0) == 0)
    def _():
        vec_sum[...] = jnp.zeros_like(vec_sum)

    upstream = grad_crossed[...]
    normed = normed1[...]
    grad_cross = norm_backward(upstream, normed, scale1[...], cross_norm[0:1])
    low = grad_cross.astype(bf16)
    grad_cross_low[...] = low
    vec_sum[2:3] += row_sum(low.astype(f32))
    vec_sum[3:4] += row_sum(upstream * normed)
    vec_sum[4:5] += row_sum(upstream)
    grad_context[...] = dot_nt(low, cross_out[...]).astype(bf16)
    attend_back(triple1, probs1, grad_context, grad_triple, 0, items, slots)
    vec_sum[0:1] += row_sum(grad_triple[:, :width].astype(f32))
    vec_sum[1:2] += row_sum(grad_triple[:, 2 * width :].astype(f32))
    grad_far[...] = dot_nt(grad_triple[:, width:], cross_proj[:, width:]).astype(bf16)
    grad_own[...] = grad_cross + dot_nt(grad_triple[:, :width], cross_proj[:, :width])


def finish_kernel(items, slots, own, far, grad_hidden, wide):
    wide[...] = own[...] + far[...].astype(f32)
    for item in range(items):
        grad_hidden[0, item] = wide[item * slots : (item + 1) * slots, :].astype(bf16)


def weight_grad_kernel(left, right, product, turned):
    @pl.when(pl.program_id(1) == 0)
    def _():
        turned[...] = left[...].T

    product[...] = dot(turned[...], right[...]).astype(bf16)


def weight_grad(left, right, at=0):
    rows, deep = left.shape
    block = HEADS * HEAD_DIM
    wide = right.shape[1] - at * block
    return pl.pallas_call(
        weight_grad_kernel,
        grid=(deep // block, wide // block),
        in_specs=[
            pl.BlockSpec((rows, block), lambda i, j: (0, i)),
            pl.BlockSpec((rows, block), lambda i, j: (0, j + at)),
        ],
        out_specs=pl.BlockSpec((block, block), lambda i, j: (i, j)),
        out_shape=jax.ShapeDtypeStruct((deep, wide), bf16),
        scratch_shapes=[pltpu.VMEM((block, rows), bf16)],
        compiler_params=pltpu.CompilerParams(vmem_limit_bytes=vmem_limit),
        cost_estimate=pl.CostEstimate(
            flops=2 * rows * deep * wide,
            bytes_accessed=2 * (rows * deep + rows * wide + deep * wide),
            transcendentals=0,
        ),
    )(left, right)


smem = pl.BlockSpec(memory_space=pltpu.SMEM)


def fixed(array):
    zeros = (0,) * array.ndim
    return pl.BlockSpec(array.shape, lambda i: zeros, pipeline_mode=pl.Buffered(1))


def rows_of(count, width):
    return pl.BlockSpec((count, width), lambda i: (i, 0))


def total_of(count, width):
    return pl.BlockSpec((count, width), lambda i: (0, 0))


def shape_of(shape, kind):
    return jax.ShapeDtypeStruct(shape, kind)


def flip(count, bit):
    return [(place, place ^ (1 << bit)) for place in range(count)]


def halve(parts, axis, bit, dim):
    mine = (lax.axis_index(axis) >> bit) & 1
    send = lax.dynamic_index_in_dim(parts, 1 - mine, dim, keepdims=False)
    keep = lax.dynamic_index_in_dim(parts, mine, dim, keepdims=False)
    return keep, lax.ppermute(send, axis, flip(lax.axis_size(axis), bit))


def scatter_sum(parts, axis, kind, other=None):
    count = lax.axis_size(axis)
    bits = count.bit_length() - 1
    stages = [(axis, bit) for bit in range(bits)]
    if other is not None:
        stages.insert(1, (other, 0))
    for number, (name, bit) in enumerate(stages):
        if name == other:
            keep, got = halve(parts, other, 0, 0)
        elif other is not None and number == 0:
            shape = parts.shape
            keep, got = halve(parts.reshape((shape[0], shape[1] // 2, 2) + shape[2:]), axis, bit, 2)
        else:
            shape = parts.shape
            keep, got = halve(parts.reshape((shape[0] // 2, 2) + shape[1:]), axis, bit, 1)
        summed = keep.astype(f32) + got.astype(f32)
        parts = summed if number == len(stages) - 1 else summed.astype(kind)
    return parts[0]


def local(
    hidden, lengths, task_flags, cotangent, cross_proj, cross_bias, cross_norm, cross_out, self_proj, self_bias,
    self_norm, self_out, ffn_up, up_bias, ffn_down, down_bias, ffn_norm,
):
    _, items, slots, width = hidden.shape
    deep = ffn_up.shape[2]
    rows = items * slots
    streams, places = lax.axis_size("stream"), lax.axis_size("dp")
    block = 8 if items % 8 == 0 else 4
    steps = items // block
    size = block * slots
    groups = items // 2
    item_spec = pl.BlockSpec((1, block, slots, width), lambda i: (0, i, 0, 0))
    probs_spec = pl.BlockSpec((block // 2, PAIRS, 4 * slots, 2 * slots), lambda i: (i, 0, 0, 0))
    row_spec = rows_of(size, width)
    scale_spec = rows_of(size, 1)
    triple_spec = rows_of(size, 3 * width)
    deep_spec = rows_of(size, deep)
    row_f32, row_bf16 = shape_of((rows, width), f32), shape_of((rows, width), bf16)
    scale_f32 = shape_of((rows, 1), f32)
    triple_bf16, deep_bf16 = shape_of((rows, 3 * width), bf16), shape_of((rows, deep), bf16)
    probs_bf16 = shape_of((groups, PAIRS, 4 * slots, 2 * slots), bf16)
    params = pltpu.CompilerParams(vmem_limit_bytes=vmem_limit)
    unit = 2 * rows * width * width

    def cost(units, count):
        return pl.CostEstimate(flops=units * unit, bytes_accessed=count, transcendentals=0)

    far, far_len = (lax.ppermute(entry, "stream", flip(streams, 0)) for entry in (hidden, lengths))

    (dense, far_dense, triple1, probs1, context1, normed1, scale1, triple2, probs2, context2, normed2, scale2) = pl.pallas_call(
        functools.partial(forward_kernel, block, slots),
        grid=(steps,),
        in_specs=[smem, smem, item_spec, item_spec]
        + [fixed(w) for w in (cross_proj, cross_bias, cross_norm, cross_out, self_proj, self_bias, self_norm, self_out)],
        out_specs=[row_spec, row_spec, triple_spec, probs_spec, row_spec, row_spec, scale_spec, triple_spec, probs_spec, row_spec, row_spec, scale_spec],
        out_shape=[row_bf16, row_bf16, triple_bf16, probs_bf16, row_bf16, row_f32, scale_f32, triple_bf16, probs_bf16, row_bf16, row_f32, scale_f32],
        scratch_shapes=[pltpu.VMEM((size, width), f32)] * 2,
        compiler_params=params,
        cost_estimate=cost(12, 30_000_000),
    )(far_len, lengths, hidden, far, cross_proj, cross_bias, cross_norm, cross_out, self_proj, self_bias, self_norm, self_out)

    output, grad_attended, attended_low, activated, grad_last_low, grad_expanded, up_sum, ffn_sum = pl.pallas_call(
        functools.partial(ffn_kernel, block, slots),
        grid=(steps,),
        in_specs=[smem, smem, row_spec, item_spec] + [fixed(w) for w in (self_norm, ffn_up, up_bias, ffn_down, down_bias, ffn_norm)],
        out_specs=[item_spec, row_spec, row_spec, deep_spec, row_spec, deep_spec, total_of(1, deep), total_of(3, width)],
        out_shape=[shape_of(hidden.shape, bf16), row_f32, row_bf16, deep_bf16, row_bf16, deep_bf16, shape_of((1, deep), f32), shape_of((3, width), f32)],
        scratch_shapes=[pltpu.VMEM((size, deep), f32), pltpu.VMEM((size, width), f32)],
        compiler_params=params,
        cost_estimate=cost(24, 30_000_000),
    )(lengths, task_flags, normed2, cotangent, self_norm, ffn_up, up_bias, ffn_down, down_bias, ffn_norm)

    grad_up = weight_grad(attended_low, grad_expanded)
    grad_down = weight_grad(activated, grad_last_low)

    grad_crossed, crossed_low, grad_mid_low, grad_triple2, self_sum = pl.pallas_call(
        functools.partial(self_back_kernel, block, slots),
        grid=(steps,),
        in_specs=[row_spec, row_spec, scale_spec, row_spec, triple_spec, probs_spec] + [fixed(w) for w in (cross_norm, self_norm, self_proj, self_out)],
        out_specs=[row_spec, row_spec, row_spec, triple_spec, total_of(5, width)],
        out_shape=[row_f32, row_bf16, row_bf16, triple_bf16, shape_of((5, width), f32)],
        scratch_shapes=[pltpu.VMEM((size, width), bf16)],
        compiler_params=params,
        cost_estimate=cost(8, 30_000_000),
    )(grad_attended, normed2, scale2, normed1, triple2, probs2, cross_norm, self_norm, self_proj, self_out)

    grad_self_proj = weight_grad(crossed_low, grad_triple2)
    grad_self_out = weight_grad(context2, grad_mid_low)

    grad_own, grad_far, grad_cross_low, grad_triple1, cross_sum = pl.pallas_call(
        functools.partial(cross_back_kernel, block, slots),
        grid=(steps,),
        in_specs=[row_spec, row_spec, scale_spec, triple_spec, probs_spec] + [fixed(w) for w in (cross_norm, cross_proj, cross_out)],
        out_specs=[row_spec, row_spec, row_spec, triple_spec, total_of(5, width)],
        out_shape=[row_f32, row_bf16, row_bf16, triple_bf16, shape_of((5, width), f32)],
        scratch_shapes=[pltpu.VMEM((size, width), bf16)],
        compiler_params=params,
        cost_estimate=cost(8, 30_000_000),
    )(grad_crossed, normed1, scale1, triple1, probs1, cross_norm, cross_proj, cross_out)

    grad_got = lax.ppermute(grad_far, "stream", flip(streams, 0))
    grad_cross_proj = jnp.concatenate([weight_grad(dense, grad_triple1[:, :width]), weight_grad(far_dense, grad_triple1, 1)], axis=1)
    grad_cross_out = weight_grad(context1, grad_cross_low)

    (grad_hidden,) = pl.pallas_call(
        functools.partial(finish_kernel, block, slots),
        grid=(steps,),
        in_specs=[row_spec, row_spec],
        out_specs=[item_spec],
        out_shape=[shape_of(hidden.shape, bf16)],
        scratch_shapes=[pltpu.VMEM((size, width), f32)],
        compiler_params=params,
        cost_estimate=cost(0, 8_000_000),
    )(grad_own, grad_got)

    def share(parts, kind=bf16):
        return scatter_sum(parts.reshape((places, parts.shape[0] // places) + parts.shape[1:]), "dp", kind)

    def share_all(parts, kind=bf16):
        return scatter_sum(
            parts.reshape((streams, places, parts.shape[0] // places // streams) + parts.shape[1:]), "dp", kind, "stream"
        )

    own_up, own_down = share(grad_up), share(grad_down)
    own_self_proj, own_self_out = share(grad_self_proj), share(grad_self_out)
    own_cross_proj, own_cross_out = share_all(grad_cross_proj), share_all(grad_cross_out)
    per = width // places
    up_rows = up_sum.reshape(places, deep // places)
    small = jnp.concatenate(
        [up_rows, ffn_sum.reshape(3, places, per).transpose(1, 0, 2).reshape(places, 3 * per),
         self_sum.reshape(5, places, per).transpose(1, 0, 2).reshape(places, 5 * per)], axis=1)
    small = share(small.reshape(places, -1), f32)[0]
    cut = deep // places
    small_up, small_vec = small[:cut], small[cut:].reshape(8, per)
    cross_small = cross_sum.reshape(5, streams * places, per // streams).transpose(1, 0, 2).reshape(streams * places, -1)
    cross_small = share_all(cross_small, f32)[0].reshape(5, per // streams)
    return (
        output,
        grad_hidden,
        own_cross_proj,
        cross_small[0:3],
        cross_small[3:5],
        own_cross_out,
        own_self_proj[None],
        small_vec[None, 3:6],
        small_vec[None, 6:8],
        own_self_out[None],
        own_up[None],
        small_up[None],
        own_down[None],
        small_vec[0][None],
        small_vec[None, 1:3],
    )


def solution(mesh):
    in_specs = (
        P("stream", "dp", None, None),
        P("stream", "dp"),
        P("stream", "dp"),
        P("stream", "dp", None, None),
        P(),
        P(),
        P(),
        P(),
        P("stream", None, None),
        P("stream", None, None),
        P("stream", None, None),
        P("stream", None, None),
        P("stream", None, None),
        P("stream", None),
        P("stream", None, None),
        P("stream", None),
        P("stream", None, None),
    )
    out_specs = (
        P("stream", "dp", None, None),
        P("stream", "dp", None, None),
        P(("stream", "dp"), None),
        P(None, ("stream", "dp")),
        P(None, ("stream", "dp")),
        P(("stream", "dp"), None),
        P("stream", "dp", None),
        P("stream", None, "dp"),
        P("stream", None, "dp"),
        P("stream", "dp", None),
        P("stream", "dp", None),
        P("stream", "dp"),
        P("stream", "dp", None),
        P("stream", "dp"),
        P("stream", None, "dp"),
    )
    return jax.shard_map(local, mesh=mesh, in_specs=in_specs, out_specs=out_specs, check_vma=False)
```

```python
import functools

import jax
import jax.numpy as jnp
from jax import lax
from jax.experimental import pallas as pl
from jax.experimental.pallas import tpu as pltpu
from jax.sharding import PartitionSpec as P

HEADS = 12
HEAD_DIM = 64
PAIRS = HEADS // 2
LANES = 2 * HEAD_DIM
TILE = 8
WIDTH = HEADS * HEAD_DIM
MESH = pl.DeviceIdType.MESH

norm_eps = 1e-06
masked_score = -1000000000.0
vmem_limit = 60 * 1024 * 1024

f32 = jnp.float32
bf16 = jnp.bfloat16


def dot(left, right):
    return jnp.dot(left, right, preferred_element_type=f32)


def dot_nt(left, right):
    return lax.dot_general(left, right, (((1,), (1,)), ((), ())), preferred_element_type=f32)


def dot_tn(left, right):
    return lax.dot_general(left, right, (((0,), (0,)), ((), ())), preferred_element_type=f32)


def norm_parts(summed):
    centred = summed - jnp.mean(summed, axis=-1, keepdims=True)
    scaled = lax.rsqrt(jnp.mean(centred * centred, axis=-1, keepdims=True) + norm_eps)
    return centred * scaled, scaled


def norm_backward(upstream, normed, scaled, gain):
    inner = upstream * gain
    return scaled * (
        inner
        - jnp.mean(inner, axis=-1, keepdims=True)
        - normed * jnp.mean(inner * normed, axis=-1, keepdims=True)
    )


def row_sum(rows):
    return jnp.sum(rows, axis=0, keepdims=True)


def gelu_parts(entries):
    size = jnp.abs(entries)
    bell = jnp.exp(entries * entries * -0.5)
    t = 1.0 / (1.0 + size * (0.3275911 * 0.7071067811865476))
    poly = t * (
        0.5 * 0.254829592
        + t
        * (
            0.5 * -0.284496736
            + t * (0.5 * 1.421413741 + t * (0.5 * -1.453152027 + t * (0.5 * 1.061405429)))
        )
    )
    tail = poly * bell
    area = jnp.where(entries >= 0.0, 1.0 - tail, tail)
    return entries * area, area + entries * bell * 0.3989422804014327


def padded(slots):
    return -(-slots // TILE) * TILE


def lane_tiles(ref, at, count):
    return jnp.concatenate([ref[at + tile, :count] for tile in range(PAIRS)], axis=1)


def to_pairs(stage, ref, at, rows, slots):
    count, high = rows.shape[0], padded(slots)
    for tile in range(PAIRS):
        stage[tile, :count] = rows[:, tile * LANES : (tile + 1) * LANES]
    for group in range(TILE // 2):
        for tile in range(PAIRS):
            ref[group, :, at + tile * LANES : at + (tile + 1) * LANES] = pair_rows(stage, tile, group, high).astype(bf16)


def pair_rows(stage, tile, group, high):
    return jnp.concatenate(
        [stage[tile, pl.ds(2 * group + item, high, stride=TILE), :] for item in range(2)], axis=0)


def put_pair(stage, tile, group, rows, high):
    for item in range(2):
        stage[tile, pl.ds(2 * group + item, high, stride=TILE), :] = rows[item * high : (item + 1) * high]


def clear_padding(stage, slots):
    stage[:, slots * TILE :] = jnp.zeros((stage.shape[0], stage.shape[1] - slots * TILE, LANES), f32)


def pair_mask(len_ref, first, high):
    shape = (2 * high, 2 * high)
    row = lax.broadcasted_iota(jnp.int32, shape, 0)
    col = lax.broadcasted_iota(jnp.int32, shape, 1)
    second = row >= high
    low = jnp.where(second, high, 0)
    end = jnp.where(second, high + len_ref[pl.ds(first + 1, 1), : 2 * high], len_ref[pl.ds(first, 1), : 2 * high])
    allowed = (col >= low) & (col < end)
    return jnp.concatenate([allowed, allowed], axis=0)


def first_head(shape):
    return lax.broadcasted_iota(jnp.int32, shape, 1) < HEAD_DIM


def head_stack(rows):
    low, zero = first_head(rows.shape), jnp.zeros_like(rows)
    return jnp.concatenate([jnp.where(low, rows, zero), jnp.where(low, zero, rows)], axis=0)


def head_merge(stacked):
    count = stacked.shape[0] // 2
    return jnp.where(first_head((count, stacked.shape[1])), stacked[:count], stacked[count:])


def batches(size):
    everything = [(group, pair) for group in range(TILE // 2) for pair in range(PAIRS)]
    return [everything[at : at + size] for at in range(0, len(everything), size)]


def head_block(ref, group, part, pair):
    return ref[group, :, part * WIDTH + pair * LANES : part * WIDTH + (pair + 1) * LANES]


def attend(triple_ref, probs_ref, context_ref, stage, len_ref, first_item, slots):
    high = padded(slots)
    ones = jnp.ones((2 * high, LANES), bf16)
    masks = [pair_mask(len_ref, first_item + 2 * group, high) for group in range(TILE // 2)]
    for batch in batches(12):
        scores = [
            jnp.where(
                masks[group],
                dot_nt(head_stack(head_block(triple_ref, group, 0, pair)), head_block(triple_ref, group, 1, pair)),
                masked_score,
            )
            for group, pair in batch
        ]
        largest = [jnp.max(entry, axis=-1, keepdims=True) for entry in scores]
        weights = [jnp.exp(entry - top).astype(bf16) for entry, top in zip(scores, largest)]
        both = [
            dot(entry, jnp.concatenate([head_block(triple_ref, group, 2, pair), ones], axis=1))
            for (group, pair), entry in zip(batch, weights)
        ]
        for (group, pair), entry, sums in zip(batch, weights, both):
            inverse = 1.0 / sums[:, LANES:]
            probs_ref[group, pair] = (entry.astype(f32) * inverse[:, : 2 * high]).astype(bf16)
            context = head_merge(sums[:, :LANES] * inverse)
            context_ref[group, :, pair * LANES : (pair + 1) * LANES] = context
            put_pair(stage, pair, group, context, high)


def attend_back(triple_ref, probs_ref, context_ref, stage, out_stage, slots):
    high = padded(slots)
    ones = jnp.ones((2 * high, LANES), bf16)
    low = first_head((2 * high, LANES))
    for batch in batches(6):
        stacks, grad_probs = [], []
        for group, pair in batch:
            grads = pair_rows(stage, pair, group, high)
            delta = -grads * context_ref[group, :, pair * LANES : (pair + 1) * LANES]
            upper = delta.astype(bf16)
            lower = pltpu.roll(delta - upper.astype(f32), HEAD_DIM, 1).astype(bf16)
            deltas = jnp.concatenate([jnp.where(low, upper, lower), jnp.where(low, lower, upper)], axis=0)
            stacks.append(head_stack(grads.astype(bf16)))
            values = head_block(triple_ref, group, 2, pair)
            grad_probs.append(
                dot_nt(jnp.concatenate([stacks[-1], deltas], axis=1), jnp.concatenate([values, ones], axis=1)))
        grad_scores = [
            (probs_ref[group, pair].astype(f32) * entry).astype(bf16) for (group, pair), entry in zip(batch, grad_probs)]
        grad_queries = [dot(entry, head_block(triple_ref, group, 1, pair)) for (group, pair), entry in zip(batch, grad_scores)]
        grad_values = [dot_tn(probs_ref[group, pair], entry) for (group, pair), entry in zip(batch, stacks)]
        grad_keys = [
            dot_tn(entry, head_stack(head_block(triple_ref, group, 0, pair))) for (group, pair), entry in zip(batch, grad_scores)]
        for at, (group, pair) in enumerate(batch):
            put_pair(out_stage, pair, group, head_merge(grad_queries[at]) * HEAD_DIM**-0.5, high)
            put_pair(out_stage, PAIRS + pair, group, grad_keys[at], high)
            put_pair(out_stage, 2 * PAIRS + pair, group, grad_values[at], high)


def across(axis, bit):
    place, weight = lax.axis_index(axis), 1 << bit
    return {axis: place + weight - 2 * weight * ((place // weight) % 2)}


def greet(partners):
    barrier = pltpu.get_barrier_semaphore()
    for partner in partners:
        pl.semaphore_signal(barrier, inc=1, device_id=partner, device_id_type=MESH)
    pl.semaphore_wait(barrier, len(partners))


def forward_kernel(
    slots, steps,
    lens, whole, hidden, cross_proj, cross_bias, cross_norm, cross_out, self_proj, self_bias, self_norm, self_out,
    dense, far_dense, triple1, probs1, contexts1, context1, normed1, scale1,
    triple2, probs2, contexts2, context2, normed2, scale2,
    wide, stage, context_stage, far, far_lens, send_sem, recv_sem,
):
    count = slots * TILE
    step = pl.program_id(0)
    partner = across("stream", 0)

    def travel(part):
        if part == steps:
            source, target = lens, far_lens
        else:
            source, target = whole.at[:, pl.ds(part * TILE, TILE)], far.at[part]
        return pltpu.make_async_remote_copy(
            src_ref=source, dst_ref=target, send_sem=send_sem.at[part], recv_sem=recv_sem.at[part],
            device_id=partner, device_id_type=MESH)

    @pl.when(step == 0)
    def _():
        greet([partner])
        travel(steps).start()
        for part in range(steps):
            travel(part).start()
        clear_padding(stage, slots)

    rows = hidden[...].astype(f32).reshape(count, WIDTH)
    wide[...] = rows
    low = rows.astype(bf16)
    dense[...] = low
    queries = (dot(low, cross_proj[:, :WIDTH]) + cross_bias[0:1]).astype(bf16).astype(f32)
    to_pairs(stage, triple1, 0, queries * HEAD_DIM**-0.5, slots)

    @pl.when(step == 0)
    def _():
        travel(steps).wait()

    for part in range(steps):

        @pl.when(step == part)
        def _():
            travel(part).wait()

    far_low = far[step].astype(f32).reshape(count, WIDTH).astype(bf16)
    far_dense[...] = far_low
    to_pairs(stage, triple1, WIDTH, dot(far_low, cross_proj[:, WIDTH : 2 * WIDTH]), slots)
    to_pairs(stage, triple1, 2 * WIDTH, dot(far_low, cross_proj[:, 2 * WIDTH :]) + cross_bias[1:2], slots)
    attend(triple1, probs1, contexts1, context_stage, far_lens, step * TILE, slots)
    low = lane_tiles(context_stage, 0, count).astype(bf16)
    context1[...] = low
    normed, scale = norm_parts(dot(low, cross_out[...]) + cross_bias[2:3] + wide[...])
    normed1[...] = normed
    scale1[...] = scale
    crossed = normed * cross_norm[0:1] + cross_norm[1:2]
    wide[...] = crossed
    low = crossed.astype(bf16)
    queries = (dot(low, self_proj[0, :, :WIDTH]) + self_bias[0, 0:1]).astype(bf16).astype(f32)
    to_pairs(stage, triple2, 0, queries * HEAD_DIM**-0.5, slots)
    to_pairs(stage, triple2, WIDTH, dot(low, self_proj[0, :, WIDTH : 2 * WIDTH]), slots)
    to_pairs(stage, triple2, 2 * WIDTH, dot(low, self_proj[0, :, 2 * WIDTH :]) + self_bias[0, 1:2], slots)
    attend(triple2, probs2, contexts2, context_stage, lens, step * TILE, slots)
    low = lane_tiles(context_stage, 0, count).astype(bf16)
    context2[...] = low
    normed, scale = norm_parts(dot(low, self_out[0]) + self_bias[0, 2:3] + wide[...])
    normed2[...] = normed
    scale2[...] = scale


def ffn_kernel(
    slots,
    live, normed2, cotangent, self_norm, ffn_up, up_bias, ffn_down, down_bias, ffn_norm,
    output, grad_attended, attended_low, activated, grad_last_low, grad_expanded, up_sum, vec_sum,
    slope,
):
    width = WIDTH
    chunks = ffn_up.shape[2] // width
    step = pl.program_id(0)

    @pl.when(step == 0)
    def _():
        up_sum[...] = jnp.zeros_like(up_sum)
        vec_sum[...] = jnp.zeros_like(vec_sum)

    attended = normed2[...] * self_norm[0, 0:1] + self_norm[0, 1:2]
    low = attended.astype(bf16)
    attended_low[...] = low
    total = attended + down_bias[...]
    for chunk in range(chunks):
        at = slice(chunk * width, (chunk + 1) * width)
        active, rise = gelu_parts(dot(low, ffn_up[0, :, at]) + up_bias[:, at])
        active = active.astype(bf16)
        activated[:, at] = active
        slope[:, at] = rise
        total = total + dot(active, ffn_down[0, at, :])
    normed, scale = norm_parts(total)
    output[...] = (normed * ffn_norm[0, 0:1] + ffn_norm[0, 1:2]).reshape(slots, TILE, WIDTH).astype(bf16)
    slot = lax.broadcasted_iota(jnp.int32, (slots, TILE, WIDTH), 0)
    alive = jnp.concatenate([live[pl.ds(pl.multiple_of(step * TILE, TILE), TILE), :]] * PAIRS, axis=1)
    upstream = jnp.where(slot < alive[None], cotangent[...].astype(f32), 0.0).reshape(slots * TILE, WIDTH)
    grad_last = norm_backward(upstream, normed, scale, ffn_norm[0, 0:1])
    grad_low = grad_last.astype(bf16)
    grad_last_low[...] = grad_low
    vec_sum[0:1] += row_sum(grad_low.astype(f32))
    vec_sum[1:2] += row_sum(upstream * normed)
    vec_sum[2:3] += row_sum(upstream)
    total = grad_last
    for chunk in range(chunks):
        at = slice(chunk * width, (chunk + 1) * width)
        grad_up = (dot_nt(grad_low, ffn_down[0, at, :]) * slope[:, at]).astype(bf16)
        grad_expanded[:, at] = grad_up
        up_sum[:, at] += row_sum(grad_up.astype(f32))
        total = total + dot_nt(grad_up, ffn_up[0, :, at])
    grad_attended[...] = total


def norm_back_sums(vec_sum, upstream, normed, scale, gain):
    @pl.when(pl.program_id(0) == 0)
    def _():
        vec_sum[...] = jnp.zeros_like(vec_sum)

    grad = norm_backward(upstream, normed, scale, gain)
    low = grad.astype(bf16)
    vec_sum[2:3] += row_sum(low.astype(f32))
    vec_sum[3:4] += row_sum(upstream * normed)
    vec_sum[4:5] += row_sum(upstream)
    return grad, low


def context_back(low, out, triple, probs, contexts, grad_triple, vec_sum, stage, out_stage, slots):
    count = slots * TILE

    @pl.when(pl.program_id(0) == 0)
    def _():
        clear_padding(stage, slots)

    grads = dot_nt(low, out).astype(bf16).astype(f32)
    for tile in range(PAIRS):
        stage[tile, :count] = grads[:, tile * LANES : (tile + 1) * LANES]
    attend_back(triple, probs, contexts, stage, out_stage, slots)
    for part in range(3):
        rows = lane_tiles(out_stage, part * PAIRS, count).astype(bf16)
        grad_triple[:, part * WIDTH : (part + 1) * WIDTH] = rows
        if part != 1:
            vec_sum[part // 2 : part // 2 + 1] += row_sum(rows.astype(f32))


def self_back_kernel(
    slots,
    grad_attended, normed2, scale2, normed1, triple2, probs2, contexts2, cross_norm, self_norm, self_proj, self_out,
    grad_crossed, crossed_low, grad_mid_low, grad_triple, vec_sum,
    stage, out_stage,
):
    grad_mid, low = norm_back_sums(vec_sum, grad_attended[...], normed2[...], scale2[...], self_norm[0, 0:1])
    grad_mid_low[...] = low
    crossed_low[...] = (normed1[...] * cross_norm[0:1] + cross_norm[1:2]).astype(bf16)
    grad_crossed[...] = grad_mid
    context_back(low, self_out[0], triple2, probs2, contexts2, grad_triple, vec_sum, stage, out_stage, slots)
    grad_crossed[...] += dot_nt(grad_triple[...], self_proj[0])


def cross_back_kernel(
    slots, steps,
    grad_crossed, normed1, scale1, triple1, probs1, contexts1, cross_norm, cross_proj, cross_out,
    grad_own, grad_far, grad_got, grad_cross_low, grad_triple, vec_sum,
    stage, out_stage, outbox, send_sem, recv_sem,
):
    step = pl.program_id(0)
    partner = across("stream", 0)

    def travel(part):
        return pltpu.make_async_remote_copy(
            src_ref=outbox.at[part], dst_ref=grad_got.at[part], send_sem=send_sem.at[part], recv_sem=recv_sem.at[part],
            device_id=partner, device_id_type=MESH)

    @pl.when(step == 0)
    def _():
        greet([partner])

    grad_cross, low = norm_back_sums(vec_sum, grad_crossed[...], normed1[...], scale1[...], cross_norm[0:1])
    grad_cross_low[...] = low
    grad_own[...] = grad_cross
    context_back(low, cross_out[...], triple1, probs1, contexts1, grad_triple, vec_sum, stage, out_stage, slots)
    rows = dot_nt(grad_triple[:, WIDTH:], cross_proj[:, WIDTH:]).astype(bf16)
    grad_far[...] = rows
    for part in range(steps - 1):

        @pl.when(step == part)
        def _():
            outbox[part] = rows
            travel(part).start()

    grad_own[...] += dot_nt(grad_triple[:, :WIDTH], cross_proj[:, :WIDTH])

    @pl.when(step == steps - 1)
    def _():
        for part in range(steps - 1):
            travel(part).wait()


def place_order(digits, share):
    starts = []
    for block in range(1 << len(digits)):
        source = 0
        for number, (axis, bit, weight) in enumerate(digits):
            mine = (lax.axis_index(axis) // (1 << bit)) % 2
            other = (block >> (len(digits) - 1 - number)) & 1
            source = source + (mine + other - 2 * mine * other) * weight
        starts.append(source * share)
    return starts


def order_matrix(digits, share):
    starts = place_order(digits, share)
    block = WIDTH // len(starts)
    source = jnp.concatenate([start + jnp.arange(block) for start in starts])
    return (source[:, None] == jnp.arange(WIDTH)[None, :]).astype(bf16)


def turn(left, digits, share, order, natural, turned):
    if order is not None:
        turned[...] = dot_nt(order, left).astype(bf16)
        return
    natural[...] = left.T
    for number, start in enumerate(place_order(digits, share)):
        turned[number * share : (number + 1) * share, :] = natural[pl.ds(pl.multiple_of(start, 16), share), :]


class Products:
    def __init__(self, plan, digits, share, lefts, rights, sums, order, natural, turned, outbox, inbox, small_out, small_in, sems):
        self.plan, self.digits, self.share = plan, digits, share
        self.lefts, self.rights, self.sums, self.order = lefts, rights, sums, order
        self.natural, self.turned, self.sems = natural, turned, sems
        self.boxes = (outbox, inbox, small_out, small_in)
        self.half = WIDTH // 2
        self.count = len(plan)
        self.total = self.count + (1 if sums else 0)

    def travel(self, at):
        outbox, inbox, small_out, small_in = self.boxes
        source, target = (outbox.at[at], inbox.at[at]) if at < self.count else (small_out, small_in)
        return pltpu.make_async_remote_copy(
            src_ref=source, dst_ref=target, send_sem=self.sems[0].at[at], recv_sem=self.sems[1].at[at],
            device_id=across("dp", 0), device_id_type=MESH)

    def block(self, at, rows):
        if at == self.count:
            return dot_nt(self.order()[rows, :], sum(ref[...] for ref in self.sums).astype(bf16))
        left, right = self.plan[at]
        return dot(self.turned[left, rows, :], self.rights[right]())

    def send(self):
        ready = set()
        for at in range(self.total):
            if at < self.count and self.plan[at][0] not in ready:
                left = self.plan[at][0]
                ready.add(left)
                order = self.order() if self.natural is None else None
                turn(self.lefts[left](), self.digits, self.share, order, self.natural, self.turned.at[left])
            product = self.block(at, slice(self.half, 2 * self.half)).astype(bf16)
            if at < self.count:
                self.boxes[0][at] = product
            else:
                self.boxes[2][...] = product
            self.travel(at).start()

    def keep(self, store):
        for at in range(self.total):
            product = self.block(at, slice(0, self.half))
            self.travel(at).wait()
            store(at, product + (self.boxes[1][at] if at < self.count else self.boxes[3][...]).astype(f32))


class Loads:
    def __init__(self, pairs, sem):
        self.copies = [pltpu.make_async_copy(source, target, sem.at[at]) for at, (source, target) in enumerate(pairs)]
        self.targets = [target for _, target in pairs]
        self.waited = set()
        for copy in self.copies:
            copy.start()

    def __getitem__(self, at):
        def read():
            if at not in self.waited:
                self.waited.add(at)
                self.copies[at].wait()
            return self.targets[at][...]

        return read


def weight_grad_kernel(plan, digits, share, stacked, sources, orders, lefts_count, sums_count, *refs):
    refs = list(refs)

    def take(count):
        out = refs[:count]
        del refs[:count]
        return out

    order = take(orders)
    operands = take(len({name for name, _ in sources}))
    sums = take(sums_count)
    kept, sent = take(2)
    natural = take(1)[0] if share % 16 == 0 else None
    turned, outbox, inbox, small_out, small_in, loaded, order_at, load_sem, send_sem, recv_sem = refs
    quarter = WIDTH // 4
    greet([across("dp", 0)])
    pairs = [(order[0], order_at)] if orders else []
    for at, (name, column) in enumerate(sources):
        pairs.append((operands[name].at[:, pl.ds(column * WIDTH, WIDTH)], loaded.at[at]))
    loads = Loads(pairs, load_sem)
    skip = len(pairs) - len(sources)
    products = Products(
        plan, digits, share, [loads[skip + at] for at in range(lefts_count)],
        [loads[skip + at] for at in range(lefts_count, len(sources))], sums, loads[0] if orders else None, natural, turned,
        outbox, inbox, small_out, small_in, (send_sem, recv_sem))

    def store(at, product):
        wide = product.shape[1]
        place = (slice(at * quarter, (at + 1) * quarter), slice(0, wide)) if stacked else (slice(0, quarter), slice(at * WIDTH, at * WIDTH + wide))
        kept[place] = product[:quarter].astype(bf16)
        sent[place] = product[quarter:].astype(bf16)

    products.send()
    products.keep(store)


def weight_grad(operands, sources, lefts_count, plan, digits, share, identity, sums=(), stacked=False, order=None):
    rows = operands[0].shape[0]
    half, quarter, count = WIDTH // 2, WIDTH // 4, len(plan)
    columns = WIDTH if stacked else count * WIDTH + (LANES if sums else 0)
    turn_rows = share % 16 == 0
    orders = [order] if sums or not turn_rows else []
    total = count + (1 if sums else 0)
    return pl.pallas_call(
        functools.partial(weight_grad_kernel, plan, digits, share, stacked, sources, len(orders), lefts_count, len(sums)),
        in_specs=[pl.BlockSpec(memory_space=pl.ANY)] * (len(orders) + len(operands)) + [pl.BlockSpec(memory_space=pltpu.VMEM)] * len(sums),
        out_specs=[pl.BlockSpec(memory_space=pltpu.VMEM)] * 2,
        out_shape=[jax.ShapeDtypeStruct((quarter * (count if stacked else 1), columns), bf16)] * 2,
        scratch_shapes=([pltpu.VMEM((WIDTH, rows), bf16)] if turn_rows else []) + [
            pltpu.VMEM((lefts_count, WIDTH, rows), bf16),
            pltpu.VMEM((count, half, WIDTH), bf16),
            pltpu.VMEM((count, half, WIDTH), bf16),
            pltpu.VMEM((half, LANES), bf16),
            pltpu.VMEM((half, LANES), bf16),
            pltpu.VMEM((len(sources), rows, WIDTH), bf16),
            pltpu.VMEM((WIDTH, WIDTH) if orders else (16, LANES), bf16),
            pltpu.SemaphoreType.DMA((len(sources) + len(orders),)),
            pltpu.SemaphoreType.DMA((total,)),
            pltpu.SemaphoreType.DMA((total,)),
        ],
        compiler_params=pltpu.CompilerParams(vmem_limit_bytes=vmem_limit, collective_id=identity, has_side_effects=True),
        cost_estimate=pl.CostEstimate(
            flops=2 * rows * WIDTH * WIDTH * (count + lefts_count),
            bytes_accessed=2 * (rows * WIDTH * len(sources) + WIDTH * columns),
            transcendentals=0,
        ),
    )(*orders, *operands, *sums)


def cross_finish_kernel(
    plan, digits, share, steps,
    order, dense, far_dense, context1, grad_triple, grad_cross_low, grad_own, grad_far, grad_got, sums,
    grad_hidden, result,
    turned, outbox, inbox, small_out, small_in, loaded, order_at, own, got, last, total, box1, box2, box3,
    load_sem, send_sem, recv_sem, send_last, recv_last, send_part, recv_part,
):
    links = [across("stream", 0), across("dp", 1), across("dp", 2)]
    greet(links + [across("dp", 0)])
    size = grad_own.shape[0] // steps
    slots = size // TILE
    columns = [grad_triple.at[:, pl.ds(part * WIDTH, WIDTH)] for part in range(3)]
    sources = [dense, columns[0], far_dense, columns[1], columns[2], context1, grad_cross_low]
    pairs = [(order, order_at)] + [(source, loaded.at[at]) for at, source in enumerate(sources)] + [(grad_own, own), (grad_got, got)]
    loads = Loads(pairs, load_sem)
    final = pltpu.make_async_remote_copy(
        src_ref=grad_far.at[pl.ds((steps - 1) * size, size)], dst_ref=last, send_sem=send_last, recv_sem=recv_last,
        device_id=links[0], device_id_type=MESH)
    final.start()
    products = Products(
        plan, digits, share, [loads[1], loads[3], loads[6]], [loads[2], loads[4], loads[5], loads[7]], [sums], loads[0], None,
        turned, outbox, inbox, small_out, small_in, (send_sem, recv_sem))
    cut = 4 * WIDTH // 3
    bounds = [(0, cut), (cut, 2 * cut), (2 * cut, total.shape[-1])]
    routes = [(0, 1, 2), (1, 2, 0), (2, 0, 1)]
    boxes = [box1, box2, box3]

    def view(part, stage, sent):
        spot = [slice(None)] * 3
        for axis in routes[part][:stage]:
            spot[axis] = 0
        spot[routes[part][stage]] = sent
        return tuple(spot) + (slice(None), slice(*bounds[part]))

    def travel(part, stage):
        wide = bounds[part][1] - bounds[part][0]
        at = 3 * part + stage
        box = boxes[stage].at[part]
        target = box.at[(slice(None),) * (3 - stage) + (slice(0, wide),)]
        return pltpu.make_async_remote_copy(
            src_ref=total.at[view(part, stage, 1)], dst_ref=target, send_sem=send_part.at[at], recv_sem=recv_part.at[at],
            device_id=links[routes[part][stage]], device_id_type=MESH)

    def store(at, product):
        wide = product.shape[1]
        rows = product.reshape(2, 2, 2, product.shape[0] // 8, wide).astype(bf16)
        total[:, :, :, :, at * WIDTH : at * WIDTH + wide] = rows
        for part in range(3):
            if at == min(part + 1, len(plan)) and part < 2 or part == 2 and at == len(plan):
                travel(part, 0).start()

    products.send()
    products.keep(store)

    def put(part, rows):
        value = own[part * size : (part + 1) * size, :] + rows.astype(f32)
        grad_hidden[:, part * TILE : (part + 1) * TILE, :] = value.reshape(slots, TILE, WIDTH).astype(bf16)

    loads[len(pairs) - 2]()
    loads[len(pairs) - 1]()
    for part in range(steps - 1):
        put(part, got[part])
    final.wait()
    put(steps - 1, last[...])
    for stage in range(3):
        for part in range(3):
            travel(part, stage).wait()
            wide = bounds[part][1] - bounds[part][0]
            spot = view(part, stage, 0)
            came = boxes[stage][(part,) + (slice(None),) * (3 - stage) + (slice(0, wide),)]
            total[spot] = (total[spot].astype(f32) + came.astype(f32)).astype(bf16)
            if stage < 2:
                travel(part, stage + 1).start()
    result[...] = total[0, 0, 0]


smem = pl.BlockSpec(memory_space=pltpu.SMEM)


def fixed(array):
    zeros = (0,) * array.ndim
    return pl.BlockSpec(array.shape, lambda i: zeros, pipeline_mode=pl.Buffered(1))


def rows_of(count, width):
    return pl.BlockSpec((count, width), lambda i: (i, 0))


def total_of(count, width):
    return pl.BlockSpec((count, width), lambda i: (0, 0))


def shape_of(shape, kind):
    return jax.ShapeDtypeStruct(shape, kind)


def flip(count, bit):
    return [(place, place ^ (1 << bit)) for place in range(count)]


def send(parts, axis, bit):
    return lax.ppermute(parts, axis, flip(lax.axis_size(axis), bit))


def add(kept, got):
    return (kept.astype(f32) + got.astype(f32)).astype(bf16)


def halve(kept, got):
    half = kept.shape[0] // 2
    return add(kept[:half], got[:half]), add(kept[half:], got[half:])


def halve_at(kept, got, axis, bit):
    mine = (lax.axis_index(axis) >> bit) & 1
    shape = (kept.shape[0] // 2, 2) + kept.shape[1:]
    kept, got = kept.reshape(shape), got.reshape(shape)

    def part(at):
        return add(lax.dynamic_index_in_dim(kept, at, 1, keepdims=False), lax.dynamic_index_in_dim(got, at, 1, keepdims=False))

    return part(mine), part(1 - mine)


def after(value, *earlier):
    return lax.optimization_barrier((value,) + earlier)


def local(
    hidden, lengths, task_flags, cotangent, cross_proj, cross_bias, cross_norm, cross_out, self_proj, self_bias,
    self_norm, self_out, ffn_up, up_bias, ffn_down, down_bias, ffn_norm,
):
    _, items, slots, width = hidden.shape
    deep = ffn_up.shape[2]
    rows = items * slots
    streams, places = lax.axis_size("stream"), lax.axis_size("dp")
    bits = places.bit_length() - 1
    steps = items // TILE
    size = TILE * slots
    high = padded(slots)
    groups = items // 2
    item_spec = pl.BlockSpec((slots, TILE, width), lambda i: (0, i, 0))
    row_spec = rows_of(size, width)
    scale_spec = rows_of(size, 1)
    wide_spec = rows_of(size, 3 * width)
    deep_spec = rows_of(size, deep)
    triple_spec = pl.BlockSpec((TILE // 2, 2 * high, 3 * width), lambda i: (i, 0, 0))
    pair_spec = pl.BlockSpec((TILE // 2, 2 * high, width), lambda i: (i, 0, 0))
    probs_spec = pl.BlockSpec((TILE // 2, PAIRS, 4 * high, 2 * high), lambda i: (i, 0, 0, 0))
    any_spec = pl.BlockSpec(memory_space=pl.ANY)
    row_f32, row_bf16 = shape_of((rows, width), f32), shape_of((rows, width), bf16)
    scale_f32 = shape_of((rows, 1), f32)
    wide_bf16, deep_bf16 = shape_of((rows, 3 * width), bf16), shape_of((rows, deep), bf16)
    triple_bf16 = shape_of((groups, 2 * high, 3 * width), bf16)
    pair_f32 = shape_of((groups, 2 * high, width), f32)
    probs_bf16 = shape_of((groups, PAIRS, 4 * high, 2 * high), bf16)
    sum_spec, sum_f32 = total_of(LANES, width), shape_of((LANES, width), f32)
    params = pltpu.CompilerParams(vmem_limit_bytes=vmem_limit)
    unit = 2 * rows * width * width
    stage = pltpu.VMEM((PAIRS, TILE * high, LANES), f32)
    out_stage = pltpu.VMEM((3 * PAIRS, TILE * high, LANES), f32)

    def remote(identity):
        return pltpu.CompilerParams(vmem_limit_bytes=vmem_limit, collective_id=identity, has_side_effects=True)

    def cost(units, count):
        return pl.CostEstimate(flops=units * unit, bytes_accessed=count, transcendentals=0)

    chunk_bits = (width * places // deep).bit_length() - 1
    share, cross_share = width // places, width // places // streams
    digits = [("dp", bit, 1 << bit) for bit in range(bits)]
    z_digits = [digits[0], digits[2], digits[1]] + digits[3:]
    cross_digits = [digits[0], ("stream", 0, places)] + digits[1:]
    order, cross_order = order_matrix(digits, share), order_matrix(cross_digits, cross_share)
    z_order = order_matrix(z_digits, share) if share % 16 else None
    lens = jnp.broadcast_to(lengths[0][:, None], (items, LANES))
    live = jnp.broadcast_to(jnp.where(task_flags[0] > 0, lengths[0], 0)[:, None], (items, LANES))
    slot_rows = jnp.transpose(hidden[0], (1, 0, 2))
    slot_cotangent = jnp.transpose(cotangent[0], (1, 0, 2))

    def down_halve(kept, got, bit):
        if bit >= chunk_bits:
            return halve_at(kept, got, "dp", bit)
        half = kept.shape[1] // 2
        return add(kept[:, :half], got[:, :half]), add(kept[:, half:], got[:, half:])

    (dense, far_dense, triple1, probs1, contexts1, context1, normed1, scale1,
     triple2, probs2, contexts2, context2, normed2, scale2) = pl.pallas_call(
        functools.partial(forward_kernel, slots, steps),
        grid=(steps,),
        in_specs=[fixed(lens), any_spec, item_spec]
        + [fixed(w) for w in (cross_proj, cross_bias, cross_norm, cross_out, self_proj, self_bias, self_norm, self_out)],
        out_specs=[row_spec, row_spec] + [triple_spec, probs_spec, pair_spec, row_spec, row_spec, scale_spec] * 2,
        out_shape=[row_bf16, row_bf16] + [triple_bf16, probs_bf16, pair_f32, row_bf16, row_f32, scale_f32] * 2,
        scratch_shapes=[
            pltpu.VMEM((size, width), f32), stage, stage,
            pltpu.VMEM((steps, slots, TILE, width), bf16),
            pltpu.VMEM((items, LANES), jnp.int32),
            pltpu.SemaphoreType.DMA((steps + 1,)),
            pltpu.SemaphoreType.DMA((steps + 1,)),
        ],
        compiler_params=remote(0),
        cost_estimate=cost(12, 40_000_000),
    )(lens, slot_rows, slot_rows, cross_proj, cross_bias, cross_norm, cross_out, self_proj, self_bias, self_norm, self_out)

    output, grad_attended, attended_low, activated, grad_last_low, grad_expanded, up_sum, ffn_sum = pl.pallas_call(
        functools.partial(ffn_kernel, slots),
        grid=(steps,),
        in_specs=[fixed(live), row_spec, item_spec] + [fixed(w) for w in (self_norm, ffn_up, up_bias, ffn_down, down_bias, ffn_norm)],
        out_specs=[item_spec, row_spec, row_spec, deep_spec, row_spec, deep_spec, total_of(1, deep), total_of(3, width)],
        out_shape=[shape_of((slots, items, width), bf16), row_f32, row_bf16, deep_bf16, row_bf16, deep_bf16, shape_of((1, deep), f32), shape_of((3, width), f32)],
        scratch_shapes=[pltpu.VMEM((size, deep), f32)],
        compiler_params=params,
        cost_estimate=cost(24, 30_000_000),
    )(live, normed2, slot_cotangent, self_norm, ffn_up, up_bias, ffn_down, down_bias, ffn_norm)

    chunks = deep // width
    down_kept, down_sent = weight_grad(
        [activated, grad_last_low], [(0, at) for at in range(chunks)] + [(1, 0)], chunks, [(at, 0) for at in range(chunks)],
        digits[:chunk_bits], deep // places, 1, stacked=True)
    attended_low, down_sent = after(attended_low, down_sent)
    up_kept, up_sent = weight_grad(
        [attended_low, grad_expanded], [(0, 0)] + [(1, at) for at in range(chunks)], 1, [(0, at) for at in range(chunks)],
        z_digits, share, 2, order=z_order)
    grad_attended, down_sent, up_sent = after(grad_attended, down_sent, up_sent)
    down_got, up_got = send(down_sent, "dp", 1), send(up_sent, "dp", 2)

    grad_crossed, crossed_low, grad_mid_low, grad_triple2, self_sum = pl.pallas_call(
        functools.partial(self_back_kernel, slots),
        grid=(steps,),
        in_specs=[row_spec, row_spec, scale_spec, row_spec, triple_spec, probs_spec, pair_spec]
        + [fixed(w) for w in (cross_norm, self_norm, self_proj, self_out)],
        out_specs=[row_spec, row_spec, row_spec, wide_spec, sum_spec],
        out_shape=[row_f32, row_bf16, row_bf16, wide_bf16, sum_f32],
        scratch_shapes=[stage, out_stage],
        compiler_params=params,
        cost_estimate=cost(8, 30_000_000),
    )(grad_attended, normed2, scale2, normed1, triple2, probs2, contexts2, cross_norm, self_norm, self_proj, self_out)

    up_small = up_sum.reshape(places, chunks, share).transpose(1, 0, 2).reshape(chunks, width)
    small = jnp.concatenate([ffn_sum, up_small], axis=0)
    small = jnp.pad(small, ((8, LANES - 8 - small.shape[0]), (0, 0)))
    rest = 1 << chunk_bits
    stack = (places // rest, rest // 4, deep // places, width)
    down_kept, down_got = down_kept.reshape(stack), down_got.reshape(stack)
    down_kept, down_sent = down_halve(down_kept, down_got, 2)
    up_kept, up_sent = halve(up_kept, up_got)
    crossed_low, down_sent, up_sent = after(crossed_low, down_sent, up_sent)
    down_got, up_got = send(down_sent, "dp", 2), send(up_sent, "dp", 1)
    self_kept, self_sent = weight_grad(
        [crossed_low, context2, grad_triple2, grad_mid_low], [(0, 0), (1, 0), (2, 0), (2, 1), (2, 2), (3, 0)], 2,
        [(0, 0), (0, 1), (0, 2), (1, 3)], digits, share, 3, (self_sum, small), order=order)
    down_kept, down_sent = down_halve(down_kept, down_got, 3)
    up_kept, up_sent = halve(up_kept, up_got)
    grad_crossed, down_sent, up_sent, self_sent = after(grad_crossed, down_sent, up_sent, self_sent)
    down_got, up_got, self_got = send(down_sent, "dp", 3), send(up_sent, "dp", 3), send(self_sent, "dp", 1)

    grad_own, grad_far, grad_got, grad_cross_low, grad_triple1, cross_sum = pl.pallas_call(
        functools.partial(cross_back_kernel, slots, steps),
        grid=(steps,),
        in_specs=[row_spec, row_spec, scale_spec, triple_spec, probs_spec, pair_spec]
        + [fixed(w) for w in (cross_norm, cross_proj, cross_out)],
        out_specs=[row_spec, row_spec, any_spec, row_spec, wide_spec, sum_spec],
        out_shape=[row_f32, row_bf16, shape_of((steps - 1, size, width), bf16), row_bf16, wide_bf16, sum_f32],
        scratch_shapes=[
            stage, out_stage,
            pltpu.VMEM((steps - 1, size, width), bf16),
            pltpu.SemaphoreType.DMA((steps - 1,)),
            pltpu.SemaphoreType.DMA((steps - 1,)),
        ],
        compiler_params=remote(5),
        cost_estimate=cost(8, 30_000_000),
    )(grad_crossed, normed1, scale1, triple1, probs1, contexts1, cross_norm, cross_proj, cross_out)

    self_kept, self_sent = halve(self_kept, self_got)
    grad_cross_low, self_sent = after(grad_cross_low, self_sent)
    self_got = send(self_sent, "dp", 2)
    half, left, parts = width // 2, width // 16, 4
    wide = 4 * width + LANES
    box = wide - 2 * (4 * width // 3)
    grad_hidden, cross_rest = pl.pallas_call(
        functools.partial(cross_finish_kernel, [(0, 0), (1, 1), (1, 2), (2, 3)], cross_digits, cross_share, steps),
        in_specs=[any_spec] * 9 + [pl.BlockSpec(memory_space=pltpu.VMEM)],
        out_specs=[pl.BlockSpec(memory_space=pltpu.VMEM)] * 2,
        out_shape=[shape_of((slots, items, width), bf16), shape_of((left, wide), bf16)],
        scratch_shapes=[
            pltpu.VMEM((3, width, rows), bf16),
            pltpu.VMEM((parts, half, width), bf16),
            pltpu.VMEM((parts, half, width), bf16),
            pltpu.VMEM((half, LANES), bf16),
            pltpu.VMEM((half, LANES), bf16),
            pltpu.VMEM((7, rows, width), bf16),
            pltpu.VMEM((width, width), bf16),
            pltpu.VMEM((rows, width), f32),
            pltpu.VMEM((steps - 1, size, width), bf16),
            pltpu.VMEM((size, width), bf16),
            pltpu.VMEM((2, 2, 2, left, wide), bf16),
            pltpu.VMEM((3, 2, 2, left, box), bf16),
            pltpu.VMEM((3, 2, left, box), bf16),
            pltpu.VMEM((3, left, box), bf16),
            pltpu.SemaphoreType.DMA((10,)),
            pltpu.SemaphoreType.DMA((parts + 1,)),
            pltpu.SemaphoreType.DMA((parts + 1,)),
            pltpu.SemaphoreType.DMA,
            pltpu.SemaphoreType.DMA,
            pltpu.SemaphoreType.DMA((9,)),
            pltpu.SemaphoreType.DMA((9,)),
        ],
        compiler_params=remote(4),
        cost_estimate=cost(7, 30_000_000),
    )(cross_order, dense, far_dense, context1, grad_triple1, grad_cross_low, grad_own, grad_far, grad_got, cross_sum)

    output, grad_hidden = (jnp.transpose(entry, (1, 0, 2))[None] for entry in (output, grad_hidden))
    self_kept, self_sent = halve(self_kept, self_got)
    cross_kept, cross_sent = cross_rest[: left // 2], cross_rest[left // 2 :]
    self_got, cross_got = send(self_sent, "dp", 3), send(cross_sent, "dp", 3)
    for bit in range(4, bits):
        up_kept, up_sent = halve(up_kept, up_got)
        up_got = send(up_sent, "dp", bit)
        self_kept, self_sent = halve(self_kept, self_got)
        self_got = send(self_sent, "dp", bit)
        cross_kept, cross_sent = halve(cross_kept, cross_got)
        cross_got = send(cross_sent, "dp", bit)
        down_kept, down_sent = down_halve(down_kept, down_got, bit)
        down_got = send(down_sent, "dp", bit)
    own_cross = cross_kept.astype(f32) + cross_got.astype(f32)
    own_up = up_kept.astype(f32) + up_got.astype(f32)
    own_down = (down_kept.astype(f32) + down_got.astype(f32)).reshape(deep // places, width)
    own_self = self_kept.astype(f32) + self_got.astype(f32)
    own_self_proj, own_self_out, self_small = own_self[:, : 3 * width], own_self[:, 3 * width : 4 * width], own_self[:, 4 * width :]
    own_cross_proj, own_cross_out, cross_small = own_cross[:, : 3 * width], own_cross[:, 3 * width : 4 * width], own_cross[:, 4 * width :]
    cross_small = cross_small[:, :5].T
    ffn_small = self_small[:, 8:11].T
    small_up = self_small[:, 11 : 11 + deep // width].T.reshape(-1)
    self_small = self_small[:, :5].T
    return (
        output,
        grad_hidden,
        own_cross_proj,
        cross_small[0:3],
        cross_small[3:5],
        own_cross_out,
        own_self_proj[None],
        self_small[None, 0:3],
        self_small[None, 3:5],
        own_self_out[None],
        own_up[None],
        small_up[None],
        own_down[None],
        ffn_small[0][None],
        ffn_small[None, 1:3],
    )


def solution(mesh):
    in_specs = (
        P("stream", "dp", None, None),
        P("stream", "dp"),
        P("stream", "dp"),
        P("stream", "dp", None, None),
        P(),
        P(),
        P(),
        P(),
        P("stream", None, None),
        P("stream", None, None),
        P("stream", None, None),
        P("stream", None, None),
        P("stream", None, None),
        P("stream", None),
        P("stream", None, None),
        P("stream", None),
        P("stream", None, None),
    )
    out_specs = (
        P("stream", "dp", None, None),
        P("stream", "dp", None, None),
        P(("stream", "dp"), None),
        P(None, ("stream", "dp")),
        P(None, ("stream", "dp")),
        P(("stream", "dp"), None),
        P("stream", "dp", None),
        P("stream", None, "dp"),
        P("stream", None, "dp"),
        P("stream", "dp", None),
        P("stream", "dp", None),
        P("stream", "dp"),
        P("stream", "dp", None),
        P("stream", "dp"),
        P("stream", None, "dp"),
    )
    return jax.shard_map(local, mesh=mesh, in_specs=in_specs, out_specs=out_specs, check_vma=False)
```

```python
import functools

import jax
import jax.numpy as jnp
from jax import lax
from jax.experimental import pallas as pl
from jax.experimental.pallas import tpu as pltpu
from jax.sharding import PartitionSpec as P

HEADS = 12
HEAD_DIM = 64
PAIRS = HEADS // 2
LANES = 2 * HEAD_DIM
TILE = 8
WIDTH = HEADS * HEAD_DIM
MESH = pl.DeviceIdType.MESH

norm_eps = 1e-06
masked_score = -1000000000.0
vmem_limit = 63 * 1024 * 1024

f32 = jnp.float32
bf16 = jnp.bfloat16


def dot(left, right):
    return jnp.dot(left, right, preferred_element_type=f32)


def dot_nt(left, right):
    return lax.dot_general(left, right, (((1,), (1,)), ((), ())), preferred_element_type=f32)


def dot_tn(left, right):
    return lax.dot_general(left, right, (((0,), (0,)), ((), ())), preferred_element_type=f32)


def norm_parts(summed):
    centred = summed - jnp.mean(summed, axis=-1, keepdims=True)
    scaled = lax.rsqrt(jnp.mean(centred * centred, axis=-1, keepdims=True) + norm_eps)
    return centred * scaled, scaled


def norm_backward(upstream, normed, scaled, gain):
    inner = upstream * gain
    return scaled * (
        inner
        - jnp.mean(inner, axis=-1, keepdims=True)
        - normed * jnp.mean(inner * normed, axis=-1, keepdims=True)
    )


def row_sum(rows):
    return jnp.sum(rows, axis=0, keepdims=True)


def gelu_parts(entries):
    size = jnp.abs(entries)
    bell = jnp.exp(entries * entries * -0.5)
    t = 1.0 / (1.0 + size * (0.3275911 * 0.7071067811865476))
    poly = t * (
        0.5 * 0.254829592
        + t
        * (
            0.5 * -0.284496736
            + t * (0.5 * 1.421413741 + t * (0.5 * -1.453152027 + t * (0.5 * 1.061405429)))
        )
    )
    tail = poly * bell
    area = jnp.where(entries >= 0.0, 1.0 - tail, tail)
    return entries * area, area + entries * bell * 0.3989422804014327


def padded(slots):
    return -(-slots // TILE) * TILE


def lane_tiles(ref, at, count):
    return jnp.concatenate([ref[at + tile, :count] for tile in range(PAIRS)], axis=1)


def to_pairs(stage, ref, at, rows, slots):
    count, high = rows.shape[0], padded(slots)
    for tile in range(PAIRS):
        stage[tile, :count] = rows[:, tile * LANES : (tile + 1) * LANES]
    for group in range(TILE // 2):
        for tile in range(PAIRS):
            ref[group, :, at + tile * LANES : at + (tile + 1) * LANES] = pair_rows(stage, tile, group, high).astype(bf16)


def pair_rows(stage, tile, group, high):
    return jnp.concatenate(
        [stage[tile, pl.ds(2 * group + item, high, stride=TILE), :] for item in range(2)], axis=0)


def put_pair(stage, tile, group, rows, high):
    for item in range(2):
        stage[tile, pl.ds(2 * group + item, high, stride=TILE), :] = rows[item * high : (item + 1) * high]


def clear_padding(stage, slots):
    stage[:, slots * TILE :] = jnp.zeros((stage.shape[0], stage.shape[1] - slots * TILE, LANES), f32)


def pair_mask(len_ref, first, high):
    shape = (2 * high, 2 * high)
    row = lax.broadcasted_iota(jnp.int32, shape, 0)
    col = lax.broadcasted_iota(jnp.int32, shape, 1)
    second = row >= high
    low = jnp.where(second, high, 0)
    end = jnp.where(second, high + len_ref[pl.ds(first + 1, 1), : 2 * high], len_ref[pl.ds(first, 1), : 2 * high])
    allowed = (col >= low) & (col < end)
    return jnp.concatenate([allowed, allowed], axis=0)


def first_head(shape):
    return lax.broadcasted_iota(jnp.int32, shape, 1) < HEAD_DIM


def head_stack(rows):
    low, zero = first_head(rows.shape), jnp.zeros_like(rows)
    return jnp.concatenate([jnp.where(low, rows, zero), jnp.where(low, zero, rows)], axis=0)


def head_merge(stacked):
    count = stacked.shape[0] // 2
    return jnp.where(first_head((count, stacked.shape[1])), stacked[:count], stacked[count:])


def batches(size):
    everything = [(group, pair) for group in range(TILE // 2) for pair in range(PAIRS)]
    return [everything[at : at + size] for at in range(0, len(everything), size)]


def head_block(ref, group, part, pair):
    return ref[group, :, part * WIDTH + pair * LANES : part * WIDTH + (pair + 1) * LANES]


def attend(triple_ref, probs_ref, context_ref, stage, len_ref, first_item, slots):
    high = padded(slots)
    ones = jnp.ones((2 * high, LANES), bf16)
    masks = [pair_mask(len_ref, first_item + 2 * group, high) for group in range(TILE // 2)]
    for batch in batches(12):
        scores = [
            jnp.where(
                masks[group],
                dot_nt(head_stack(head_block(triple_ref, group, 0, pair)), head_block(triple_ref, group, 1, pair)),
                masked_score,
            )
            for group, pair in batch
        ]
        largest = [jnp.max(entry, axis=-1, keepdims=True) for entry in scores]
        weights = [jnp.exp(entry - top).astype(bf16) for entry, top in zip(scores, largest)]
        both = [
            dot(entry, jnp.concatenate([head_block(triple_ref, group, 2, pair), ones], axis=1))
            for (group, pair), entry in zip(batch, weights)
        ]
        for (group, pair), entry, sums in zip(batch, weights, both):
            inverse = 1.0 / sums[:, LANES:]
            probs_ref[group, pair] = (entry.astype(f32) * inverse[:, : 2 * high]).astype(bf16)
            context = head_merge(sums[:, :LANES] * inverse)
            context_ref[group, :, pair * LANES : (pair + 1) * LANES] = context
            put_pair(stage, pair, group, context, high)


def attend_back(triple_ref, probs_ref, context_ref, stage, out_stage, slots):
    high = padded(slots)
    ones = jnp.ones((2 * high, LANES), bf16)
    low = first_head((2 * high, LANES))
    for batch in batches(6):
        stacks, grad_probs = [], []
        for group, pair in batch:
            grads = pair_rows(stage, pair, group, high)
            delta = -grads * context_ref[group, :, pair * LANES : (pair + 1) * LANES]
            upper = delta.astype(bf16)
            lower = pltpu.roll(delta - upper.astype(f32), HEAD_DIM, 1).astype(bf16)
            deltas = jnp.concatenate([jnp.where(low, upper, lower), jnp.where(low, lower, upper)], axis=0)
            stacks.append(head_stack(grads.astype(bf16)))
            values = head_block(triple_ref, group, 2, pair)
            grad_probs.append(
                dot_nt(jnp.concatenate([stacks[-1], deltas], axis=1), jnp.concatenate([values, ones], axis=1)))
        grad_scores = [
            (probs_ref[group, pair].astype(f32) * entry).astype(bf16) for (group, pair), entry in zip(batch, grad_probs)]
        grad_queries = [dot(entry, head_block(triple_ref, group, 1, pair)) for (group, pair), entry in zip(batch, grad_scores)]
        grad_values = [dot_tn(probs_ref[group, pair], entry) for (group, pair), entry in zip(batch, stacks)]
        grad_keys = [
            dot_tn(entry, head_stack(head_block(triple_ref, group, 0, pair))) for (group, pair), entry in zip(batch, grad_scores)]
        for at, (group, pair) in enumerate(batch):
            put_pair(out_stage, pair, group, head_merge(grad_queries[at]) * HEAD_DIM**-0.5, high)
            put_pair(out_stage, PAIRS + pair, group, grad_keys[at], high)
            put_pair(out_stage, 2 * PAIRS + pair, group, grad_values[at], high)


def across(axis, bit):
    place, weight = lax.axis_index(axis), 1 << bit
    return {axis: place + weight - 2 * weight * ((place // weight) % 2)}


def own_bit(axis, bit):
    return (lax.axis_index(axis) // (1 << bit)) % 2


def greet(partners):
    barrier = pltpu.get_barrier_semaphore()
    for partner in partners:
        pl.semaphore_signal(barrier, inc=1, device_id=partner, device_id_type=MESH)
    pl.semaphore_wait(barrier, len(partners))


def remote_copy(source, target, sems, at, partner):
    return pltpu.make_async_remote_copy(
        src_ref=source, dst_ref=target, send_sem=sems[0].at[at], recv_sem=sems[1].at[at],
        device_id=partner, device_id_type=MESH)


def row_slices(slots):
    step = 6 if slots % 6 == 0 else slots
    return [slice(at * TILE, (at + step) * TILE) for at in range(0, slots, step)]


def fold(rows):
    return jnp.sum(rows.reshape(rows.shape[0] // TILE, TILE, rows.shape[1]), axis=0)


def norm_rows(wide, normed_ref, scale_ref, gain, shift, low, slots):
    for rows in row_slices(slots):
        normed, scale = norm_parts(wide[rows])
        normed_ref[rows] = normed
        scale_ref[rows] = scale
        result = normed * gain + shift
        wide[rows] = result
        if low is not None:
            low[rows] = result.astype(bf16)


def norm_back_rows(upstream_ref, normed_ref, scale_ref, gain, grad_ref, low_ref, vec_sum, slots):
    sums = [0.0, 0.0, 0.0]
    for rows in row_slices(slots):
        upstream, normed = upstream_ref[rows], normed_ref[rows]
        grad = norm_backward(upstream, normed, scale_ref[rows], gain)
        low = grad.astype(bf16)
        grad_ref[rows] = grad
        low_ref[rows] = low
        sums = [total + fold(part) for total, part in zip(sums, (low.astype(f32), upstream * normed, upstream))]
    for at, total in enumerate(sums):
        vec_sum[2 + at : 3 + at] += row_sum(total)


def forward_kernel(
    slots, steps,
    lengths, whole, hidden, cross_proj_at, cross_out_at, self_proj_at, self_out_at, cross_bias, cross_norm, self_bias, self_norm,
    dense, far_dense, triple1, probs1, contexts1, context1, normed1, scale1,
    triple2, probs2, contexts2, context2, normed2, scale2,
    wide, low, stage, context_stage, far, lens, far_lens, cross_proj, cross_out, self_proj, self_out, send_sem, recv_sem, load_sem,
):
    count = slots * TILE
    step = pl.program_id(0)
    partner = across("stream", 0)
    sources = [cross_proj_at, cross_out_at, self_proj_at.at[0], self_out_at.at[0]]
    loads = [
        pltpu.make_async_copy(source, target, load_sem.at[at])
        for at, (source, target) in enumerate(zip(sources, [cross_proj, cross_out, self_proj, self_out]))
    ]

    def travel(part):
        if part == steps:
            source, target = lens, far_lens
        else:
            source, target = whole.at[:, pl.ds(part * TILE, TILE)], far.at[part]
        return remote_copy(source, target, (send_sem, recv_sem), part, partner)

    @pl.when(step == 0)
    def _():
        loads[0].start()
        for item in range(lens.shape[0]):
            lens[item : item + 1] = jnp.full((1, LANES), lengths[0, item], jnp.int32)
        greet([partner])
        travel(steps).start()
        for part in range(steps):
            travel(part).start()
        for load in loads[1:]:
            load.start()
        clear_padding(stage, slots)
        loads[0].wait()

    rows = hidden[...].astype(f32).reshape(count, WIDTH)
    wide[...] = rows
    dense[...] = rows.astype(bf16)
    queries = (dot(dense[...], cross_proj[:, :WIDTH]) + cross_bias[0:1]).astype(bf16).astype(f32)
    to_pairs(stage, triple1, 0, queries * HEAD_DIM**-0.5, slots)

    @pl.when(step == 0)
    def _():
        travel(steps).wait()
        for load in loads[1:]:
            load.wait()

    for part in range(steps):

        @pl.when(step == part)
        def _():
            travel(part).wait()

    far_dense[...] = far[step].astype(f32).reshape(count, WIDTH).astype(bf16)
    to_pairs(stage, triple1, WIDTH, dot(far_dense[...], cross_proj[:, WIDTH : 2 * WIDTH]), slots)
    to_pairs(stage, triple1, 2 * WIDTH, dot(far_dense[...], cross_proj[:, 2 * WIDTH :]) + cross_bias[1:2], slots)
    attend(triple1, probs1, contexts1, context_stage, far_lens, step * TILE, slots)
    context1[...] = lane_tiles(context_stage, 0, count).astype(bf16)
    wide[...] += dot(context1[...], cross_out[...]) + cross_bias[2:3]
    norm_rows(wide, normed1, scale1, cross_norm[0:1], cross_norm[1:2], low, slots)
    queries = (dot(low[...], self_proj[:, :WIDTH]) + self_bias[0, 0:1]).astype(bf16).astype(f32)
    to_pairs(stage, triple2, 0, queries * HEAD_DIM**-0.5, slots)
    to_pairs(stage, triple2, WIDTH, dot(low[...], self_proj[:, WIDTH : 2 * WIDTH]), slots)
    to_pairs(stage, triple2, 2 * WIDTH, dot(low[...], self_proj[:, 2 * WIDTH :]) + self_bias[0, 1:2], slots)
    attend(triple2, probs2, contexts2, context_stage, lens, step * TILE, slots)
    context2[...] = lane_tiles(context_stage, 0, count).astype(bf16)
    wide[...] += dot(context2[...], self_out[...]) + self_bias[0, 2:3]
    for rows in row_slices(slots):
        normed, scale = norm_parts(wide[rows])
        normed2[rows] = normed
        scale2[rows] = scale


def order_rows(digits, share):
    shape = (WIDTH, WIDTH)
    row, col = (lax.broadcasted_iota(jnp.int32, shape, dim) for dim in range(2))
    block, spot = col // share, 0
    for axis, bit, weight in digits:
        mine, other = own_bit(axis, bit), (block // weight) % 2
        spot = 2 * spot + mine + other - 2 * mine * other
    return jnp.where(row == spot * share + col % share, 1.0, 0.0).astype(bf16)


def own_first(digits, block):
    spot = 0
    for axis, bit, weight in digits:
        mine, other = own_bit(axis, bit), (block // weight) % 2
        spot = 2 * spot + mine + other - 2 * mine * other
    return spot


class Products:
    def __init__(self, share, both, inbox, sems, wide=None, order=None):
        self.share, self.both, self.inbox, self.sems, self.wide, self.order = share, both, inbox, sems, wide, order
        self.half = WIDTH // 2
        self.small = self.share % (TILE if wide is not None else 2 * TILE) != 0

    def travel(self, at):
        return remote_copy(self.both.at[at, pl.ds(self.half, self.half)], self.inbox.at[at], self.sems, at, across("dp", 0))

    def put(self, at, product, digits):
        columns = slice(0, product.shape[1])
        if self.small:
            self.both[at, :, columns] = dot(order_rows(digits, self.share), product.astype(bf16)).astype(bf16)
        elif self.wide is not None:
            for block in range(WIDTH // self.share):
                spot = pl.multiple_of(own_first(digits, block) * self.share, TILE)
                self.wide[pl.ds(spot, self.share), columns] = product[block * self.share : (block + 1) * self.share]
            self.both[at, :, columns] = self.wide[:, columns].astype(bf16)
        else:
            for block in range(WIDTH // self.share):
                spot = pl.multiple_of(own_first(digits, block) * self.share, 2 * TILE)
                self.both[at, pl.ds(spot, self.share), columns] = product[block * self.share : (block + 1) * self.share].astype(bf16)
        self.travel(at).start()

    def send(self, at, left, right, digits):
        self.put(at, dot_tn(left, right), digits)

    def send_sums(self, at, sums, digits):
        self.put(at, sums.T, digits)

    def keep(self, at, wide=WIDTH):
        self.travel(at).wait()
        return self.both[at, : self.half, :wide].astype(f32) + self.inbox[at, :, :wide].astype(f32)


class Halving:
    def __init__(self, now, boxes, sems, base, partners, first=None):
        self.now, self.boxes, self.sems, self.base, self.partners, self.first = now, boxes, sems, base, partners, first

    def travel(self, stage):
        box = self.boxes[stage]
        source = self.first
        if stage > 0 or source is None:
            source = self.now.at[pl.ds(box.shape[0], box.shape[0])]
        return remote_copy(source, box, self.sems, self.base + stage, self.partners[stage])

    def start(self, stage):
        self.travel(stage).start()

    def total(self, stage):
        self.travel(stage).wait()
        box = self.boxes[stage]
        return self.now[: box.shape[0]].astype(f32) + box[...].astype(f32)

    def finish(self, stage):
        self.now[: self.boxes[stage].shape[0]] = self.total(stage).astype(bf16)


def ffn_rows(
    slots, step, live, normed2, cotangent, self_norm, ffn_up, up_bias, ffn_down, down_bias, ffn_norm, down_load,
    output, grad_attended, attended_low, activated, grad_last_low, grad_expanded, up_sum, vec_sum, slope, wide,
):
    count = slots * TILE
    here = pl.ds(pl.multiple_of(step * count, count), count)
    chunks = ffn_up.shape[1] // WIDTH
    attended = normed2[...] * self_norm[0, 0:1] + self_norm[0, 1:2]
    attended_low[here] = attended.astype(bf16)
    wide[...] = attended + down_bias[...]
    parts = [slice(chunk * WIDTH, (chunk + 1) * WIDTH) for chunk in range(chunks)]

    def rise(part):
        return dot(attended_low[here], ffn_up[:, part]) + up_bias[:, part]

    entries = rise(parts[0])
    for number, part in enumerate(parts):
        later = rise(parts[number + 1]) if number + 1 < chunks else None
        active, steep = gelu_parts(entries)
        activated[here, part] = active.astype(bf16)
        slope[:, part] = steep
        if number == 0:

            @pl.when(step == 0)
            def _():
                down_load.wait()

        wide[...] += dot(activated[here, part], ffn_down[part, :])
        entries = later
    each = slots // len(row_slices(slots))
    sums = [0.0, 0.0, 0.0]
    alive = jnp.concatenate([live[...]] * PAIRS, axis=1)
    for number, rows in enumerate(row_slices(slots)):
        spots = slice(number * each, (number + 1) * each)
        shape = (each, TILE, WIDTH)
        normed, scale = norm_parts(wide[rows])
        output[spots] = (normed * ffn_norm[0, 0:1] + ffn_norm[0, 1:2]).reshape(shape).astype(bf16)
        slot = lax.broadcasted_iota(jnp.int32, shape, 0) + number * each
        upstream = jnp.where(slot < alive[None], cotangent[spots].astype(f32), 0.0).reshape(each * TILE, WIDTH)
        grad = norm_backward(upstream, normed, scale, ffn_norm[0, 0:1])
        low = grad.astype(bf16)
        wide[rows] = grad
        grad_last_low[pl.ds(pl.multiple_of(step * count + number * each * TILE, each * TILE), each * TILE)] = low
        sums = [total + fold(part) for total, part in zip(sums, (low.astype(f32), upstream * normed, upstream))]
    for at, total in enumerate(sums):
        vec_sum[at : at + 1] += row_sum(total)
    grad_low = grad_last_low[here]
    total = wide[...]
    for part in parts:
        grad_up = (dot_nt(grad_low, ffn_down[part, :]) * slope[:, part]).astype(bf16)
        grad_expanded[here, part] = grad_up
        up_sum[:, part] += row_sum(grad_up.astype(f32))
        total = total + dot_nt(grad_up, ffn_up[:, part])
    grad_attended[...] = total


def ffn_kernel(
    slots, steps, down_digits, down_share, up_digits, up_share, chunk_digits,
    lengths, flags, normed2, cotangent, ffn_up_at, ffn_down_at, self_norm, up_bias, down_bias, ffn_norm,
    output, grad_attended, up_sum, vec_sum, down_kept, down_sent, up_kept, up_sent,
    ffn_up, ffn_down, attended_low, activated, grad_last_low, grad_expanded, slope, wide, live,
    down_both, down_in, up_both, up_in, load_sem, down_send, down_recv, up_send, up_recv,
):
    step = pl.program_id(0)
    chunks = ffn_up.shape[1] // WIDTH
    loads = [
        pltpu.make_async_copy(ffn_up_at.at[0], ffn_up, load_sem.at[0]),
        pltpu.make_async_copy(ffn_down_at.at[0], ffn_down, load_sem.at[1]),
    ]

    @pl.when(step == 0)
    def _():
        for load in loads:
            load.start()
        greet([across("dp", 0)])
        up_sum[...] = jnp.zeros_like(up_sum)
        vec_sum[...] = jnp.zeros_like(vec_sum)
        loads[0].wait()

    @pl.when(step < steps)
    def _():
        for item in range(TILE):
            count = jnp.where(flags[0, step * TILE + item] > 0, lengths[0, step * TILE + item], 0)
            live[item : item + 1] = jnp.full((1, LANES), count, jnp.int32)
        ffn_rows(
            slots, step, live, normed2, cotangent, self_norm, ffn_up, up_bias, ffn_down, down_bias, ffn_norm, loads[1],
            output, grad_attended, attended_low, activated, grad_last_low, grad_expanded, up_sum, vec_sum, slope, wide)

    @pl.when(step == steps)
    def _():
        quarter = WIDTH // 4
        down = Products(down_share, down_both, down_in, (down_send, down_recv))
        up = Products(up_share, up_both, up_in, (up_send, up_recv))
        inner = quarter // down_share

        def keep_down(chunk):
            product = down.keep(chunk).astype(bf16)
            place = own_first(chunk_digits, chunk)
            for piece in range(inner):
                spot = pl.ds(pl.multiple_of((piece * chunks + place) * down_share, 16), down_share)
                from_own = slice(piece * down_share, (piece + 1) * down_share)
                from_other = slice(quarter + piece * down_share, quarter + (piece + 1) * down_share)
                down_kept[spot, :] = product[from_own]
                down_sent[spot, :] = product[from_other]

        def keep_up(chunk):
            product = up.keep(chunk).astype(bf16)
            at = slice(chunk * WIDTH, (chunk + 1) * WIDTH)
            up_kept[:, at] = product[:quarter]
            up_sent[:, at] = product[quarter:]

        for chunk in range(chunks):
            down.send(chunk, activated[:, chunk * WIDTH : (chunk + 1) * WIDTH], grad_last_low[...], down_digits)
            if chunk > 1:
                keep_down(chunk - 2)
        for chunk in range(chunks):
            up.send(chunk, attended_low[...], grad_expanded[:, chunk * WIDTH : (chunk + 1) * WIDTH], up_digits)
            if chunk < 2:
                keep_down(chunks - 2 + chunk)
            else:
                keep_up(chunk - 2)
        keep_up(chunks - 2)
        keep_up(chunks - 1)


def context_back(low, out, triple, probs, contexts, grad_triple, here, vec_sum, stage, out_stage, slots):
    count = slots * TILE
    grads = dot_nt(low, out).astype(bf16).astype(f32)
    for tile in range(PAIRS):
        stage[tile, :count] = grads[:, tile * LANES : (tile + 1) * LANES]
    attend_back(triple, probs, contexts, stage, out_stage, slots)
    for part in range(3):
        rows = lane_tiles(out_stage, part * PAIRS, count).astype(bf16)
        grad_triple[here, part * WIDTH : (part + 1) * WIDTH] = rows
        if part != 1:
            vec_sum[part // 2 : part // 2 + 1] += row_sum(rows.astype(f32))


def self_kernel(
    slots, steps, digits, z_digits, share,
    grad_attended, normed2, scale2, normed1, triple2, probs2, contexts2,
    cross_norm, self_norm, ffn_sum, up_sum, self_proj_at, self_out_at, context_at,
    down_kept, down_sent, up_kept, up_sent,
    grad_crossed, down_half, up_half, self_kept, self_sent,
    stage, out_stage, self_proj, self_out, context, crossed_low, grad_mid_low, grad_triple, vec_sum,
    both, inbox,
    down_now, down_box1, down_box2, up_now, up_box1, up_box2, load_sem, send_sem, recv_sem, sum_send, sum_recv,
):
    step = pl.program_id(0)
    count = slots * TILE
    here = pl.ds(pl.multiple_of(step * count, count), count)
    near, next_one = across("dp", 1), across("dp", 2)
    sums = (sum_send, sum_recv)
    early, late = [], []
    for number, (now, boxes, route, sent) in enumerate((
        (down_now, (down_box1, down_box2), [near, next_one], down_sent), (up_now, (up_box1, up_box2), [next_one, near], up_sent),
    )):
        cut = now.shape[1] // 2
        for place, group in enumerate((early, late)):
            columns = pl.ds(place * cut, cut)
            group.append(Halving(
                now.at[:, columns], [box.at[:, columns] for box in boxes], sums, 4 * number + 2 * place, route, sent.at[:, columns]))
    pairs = [
        (self_out_at.at[0], self_out), (self_proj_at.at[0], self_proj), (down_kept, down_now), (up_kept, up_now),
        (context_at, context),
    ]
    loads = [pltpu.make_async_copy(source, target, load_sem.at[at]) for at, (source, target) in enumerate(pairs)]

    @pl.when(step == 0)
    def _():
        loads[0].start()
        greet([across("dp", 0), near, next_one])
        for part in early:
            part.start(0)
        for load in loads[1:]:
            load.start()
        vec_sum[...] = jnp.zeros_like(vec_sum)
        clear_padding(stage, slots)
        loads[0].wait()
        loads[1].wait()

    @pl.when(step < steps)
    def _():
        norm_back_rows(grad_attended, normed2, scale2, self_norm[0, 0:1], grad_crossed, grad_mid_low.at[here], vec_sum, slots)
        crossed_low[here] = (normed1[...] * cross_norm[0:1] + cross_norm[1:2]).astype(bf16)
        context_back(grad_mid_low[here], self_out[...], triple2, probs2, contexts2, grad_triple, here, vec_sum, stage, out_stage, slots)
        grad_crossed[...] += dot_nt(grad_triple[here], self_proj[...])

    @pl.when(step == 0)
    def _():
        for part in late:
            part.start(0)

    @pl.when(step == steps - 2)
    def _():
        loads[2].wait()
        loads[3].wait()
        for part in early:
            part.finish(0)
            part.start(1)

    @pl.when(step == steps)
    def _():
        loads[4].wait()
        vec_sum[8:11] = ffn_sum[...]
        chunks = up_sum.shape[1] // WIDTH
        for chunk in range(chunks):
            vec_sum[16 + chunk : 17 + chunk] = up_sum[:, chunk * WIDTH : (chunk + 1) * WIDTH]
        quarter = WIDTH // 4
        products = Products(share, both, inbox, (send_sem, recv_sem))
        orders = [digits, digits, digits, z_digits, z_digits]

        def keep(at, wide=WIDTH):
            product = products.keep(at, wide).astype(bf16)
            columns = slice(at * WIDTH, at * WIDTH + wide)
            self_kept[:, columns] = product[:quarter]
            self_sent[:, columns] = product[quarter:]

        for part in range(3):
            products.send(part, crossed_low[...], grad_triple[:, part * WIDTH : (part + 1) * WIDTH], orders[part])
            if part > 0:
                keep(part - 1)
        products.send(3, context[...], grad_mid_low[...], orders[3])
        keep(2)
        turned = vec_sum[...].T
        lane = lax.broadcasted_iota(jnp.int32, (share, LANES), 1)
        wide = [jnp.broadcast_to(turned[:, 16 + chunk : 17 + chunk], (WIDTH, LANES)) for chunk in range(chunks)]
        pieces = []
        for place in range(WIDTH // share):
            piece = turned[place * share : (place + 1) * share]
            for column in range(chunks):
                source = (place * chunks + column) * share
                rows = wide[source // WIDTH][source % WIDTH : source % WIDTH + share]
                piece = jnp.where(lane == 11 + column, rows, piece)
            pieces.append(piece)
        products.put(4, jnp.concatenate(pieces, axis=0), orders[4])
        keep(3)
        keep(4, LANES)
        for part in late:
            part.finish(0)
        for part in early:
            part.finish(1)
        down_half[...] = down_now[...]
        up_half[...] = up_now[...]


def cross_kernel(
    slots, steps, digits, share, finish,
    grad_crossed, normed1, scale1, triple1, probs1, contexts1,
    cross_norm, cross_proj_at, cross_out_at, dense_at, far_at, context_at,
    down_at, up_at, self_kept, self_sent,
    grad_hidden, own_down, own_up, self_result, cross_result,
    stage, out_stage, cross_proj, cross_out, lefts, grad_cross_low, grad_triple, grad_own, vec_sum,
    dx_out, dx_in, both, inbox, wide, total, box1, box2, box3, last_out, last_in,
    down_now, down_box1, down_box2, up_now, up_box1, up_box2, self_now, self_box1, self_box2, self_box3,
    load_sem, send_sem, recv_sem, dx_send, dx_recv, sum_send, sum_recv, part_send, part_recv, out_sem,
):
    step = pl.program_id(0)
    count = slots * TILE
    here = pl.ds(pl.multiple_of(step * count, count), count)
    links = [across("stream", 0), across("dp", 1), across("dp", 2)]
    sums = (sum_send, sum_recv)
    last = across("dp", 3)
    early, late = [], []
    for number, (now, boxes, route) in enumerate((
        (down_now, (down_box1, down_box2), [links[2], last]), (up_now, (up_box1, up_box2), [links[1], last]),
    )):
        cut = now.shape[1] // 2
        high = now.shape[0] // 2
        early.append(Halving(
            now.at[pl.ds(0, high), pl.ds(0, cut)], [boxes[1].at[:, pl.ds(0, cut)]], sums, 8 + number, route[1:]))
        columns = pl.ds(cut, cut)
        late.append(Halving(now.at[:, columns], [box.at[:, columns] for box in boxes], sums, 10 + 2 * number, route))
    middle = 3 * WIDTH
    own = []
    for number, (columns, route) in enumerate((
        (pl.ds(0, middle), [links[1], links[2], last]), (pl.ds(middle, self_now.shape[1] - middle), [links[2], links[1], last]),
    )):
        boxes = [box.at[:, columns] for box in (self_box1, self_box2, self_box3)]
        own.append(Halving(self_now.at[:, columns], boxes, sums, 3 * number, route, self_sent.at[:, columns]))
    pairs = [
        (cross_out_at, cross_out), (cross_proj_at, cross_proj), (down_at, down_now), (up_at, up_now), (self_kept, self_now),
        (dense_at, lefts.at[0]), (far_at, lefts.at[1]), (context_at, lefts.at[0]),
    ]
    loads = [pltpu.make_async_copy(source, target, load_sem.at[at]) for at, (source, target) in enumerate(pairs)]

    def travel(part):
        return remote_copy(dx_out.at[part], dx_in.at[part], (dx_send, dx_recv), part, links[0])

    @pl.when(step == 0)
    def _():
        for at in (0, 2, 3, 1, 4):
            loads[at].start()
        greet(links + [last, across("dp", 0)])
        loads[2].wait()
        loads[3].wait()
        for part in early + late + own:
            part.start(0)
        for at in (5, 6):
            loads[at].start()
        vec_sum[...] = jnp.zeros_like(vec_sum)
        clear_padding(stage, slots)
        loads[0].wait()
        loads[1].wait()

    @pl.when(step < steps)
    def _():
        norm_back_rows(grad_crossed, normed1, scale1, cross_norm[0:1], grad_own.at[here], grad_cross_low.at[here], vec_sum, slots)
        context_back(grad_cross_low[here], cross_out[...], triple1, probs1, contexts1, grad_triple, here, vec_sum, stage, out_stage, slots)
        dx_out[step] = dot_nt(grad_triple[here, WIDTH:], cross_proj[:, WIDTH:]).reshape(slots, TILE, WIDTH).astype(bf16)
        travel(step).start()
        grad_own[here] += dot_nt(grad_triple[here, :WIDTH], cross_proj[:, :WIDTH])

    @pl.when(step == steps - 2)
    def _():
        for part in late:
            part.finish(0)
            part.start(1)

    @pl.when(step == steps)
    def _():
        for at in range(4, len(loads) - 1):
            loads[at].wait()
        for part in own:
            part.finish(0)
            part.start(1)
        products = Products(share, both, inbox, (send_sem, recv_sem), wide)
        cut = 4 * WIDTH // 3
        bounds = [(0, cut), (cut, 2 * cut), (2 * cut, total.shape[-1])]
        routes = [(0, 1, 2), (1, 0, 2), (0, 1, 2)]
        boxes = [box1, box2, box3]

        def view(part, stage, sent):
            spot = [slice(None)] * 3
            for axis in routes[part][:stage]:
                spot[axis] = 0
            spot[routes[part][stage]] = sent
            return tuple(spot) + (slice(None), slice(*bounds[part]))

        def box_view(part, stage):
            wide = bounds[part][1] - bounds[part][0]
            return (part,) + (slice(None),) * (3 - stage) + (slice(0, wide),)

        def hop(part, stage):
            return remote_copy(
                total.at[view(part, stage, 1)], boxes[stage].at[box_view(part, stage)], (part_send, part_recv),
                3 * part + stage, links[routes[part][stage]])

        def keep(at, wide=WIDTH):
            product = products.keep(at, wide)
            total[:, :, :, :, at * WIDTH : at * WIDTH + wide] = product.reshape(2, 2, 2, product.shape[0] // 8, wide).astype(bf16)

        products.send(0, lefts[0], grad_triple[:, :WIDTH], digits)
        loads[7].start()
        products.send(1, lefts[1], grad_triple[:, WIDTH : 2 * WIDTH], digits)
        keep(0)
        products.send(2, lefts[1], grad_triple[:, 2 * WIDTH :], digits)
        keep(1)
        hop(0, 0).start()
        loads[7].wait()
        products.send(3, lefts[0], grad_cross_low[...], digits)
        keep(2)
        hop(1, 0).start()
        products.send_sums(4, vec_sum[...], digits)
        keep(3)
        keep(4, LANES)
        hop(2, 0).start()
        for part in own:
            part.finish(1)
            part.start(2)
        def leave(part):
            return pltpu.make_async_copy(dx_out.at[part], grad_hidden.at[:, pl.ds(part * TILE, TILE)], out_sem.at[part])

        def write(part):
            travel(part).wait()
            value = grad_own[part * count : (part + 1) * count].reshape(slots, TILE, WIDTH) + dx_in[part].astype(f32)
            dx_out[part] = value.astype(bf16)
            leave(part).start()

        for part in range(steps):
            write(part)
        last_rows = total.shape[3] // 2

        def last_hop(part):
            columns = pl.ds(bounds[part][0], bounds[part][1] - bounds[part][0])
            return remote_copy(last_out.at[:, columns], last_in.at[:, columns], (part_send, part_recv), 9 + part, last)

        kept = []
        for stage_at in range(3):
            for part in range(3):
                hop(part, stage_at).wait()
                spot = view(part, stage_at, 0)
                summed = total[spot].astype(f32) + boxes[stage_at][box_view(part, stage_at)].astype(f32)
                if stage_at < 2:
                    total[spot] = summed.astype(bf16)
                    hop(part, stage_at + 1).start()
                elif not finish:
                    cross_result[:, slice(*bounds[part])] = summed
                else:
                    kept.append(summed[:last_rows])
                    gap = jnp.zeros((last_out.shape[0] - last_rows, summed.shape[1]), f32)
                    last_out[:, slice(*bounds[part])] = jnp.concatenate([summed[last_rows:], gap], axis=0).astype(bf16)
                    last_hop(part).start()
        for first, second, result in zip(early, late, (own_down, own_up)):
            cut = result.shape[1] // 2
            result[:, :cut] = first.total(0)
            result[:, cut:] = second.total(1)
        self_result[...] = jnp.concatenate([part.total(2) for part in own], axis=1)
        if finish:
            for part in range(3):
                last_hop(part).wait()
            cross_result[...] = jnp.concatenate(kept, axis=1) + last_in[...].astype(f32)[:last_rows]
        for part in range(steps):
            leave(part).wait()


def unpack_kernel(
    output, grad_hidden, own_down, own_up, own_self, own_cross,
    output_to, grad_hidden_to, own_down_to, own_up_to, self_proj, self_out, self_bias, self_norm, down_bias, ffn_norm, up_bias,
    cross_proj, cross_out, cross_bias, cross_norm,
):
    for source, target in zip((output, grad_hidden, own_down, own_up), (output_to, grad_hidden_to, own_down_to, own_up_to)):
        target[...] = source[...]
    for source, wide, narrow in ((own_self, self_proj, self_out), (own_cross, cross_proj, cross_out)):
        wide[...] = source[:, : 3 * WIDTH]
        narrow[...] = source[:, 3 * WIDTH : 4 * WIDTH]
    small = own_self[:, 4 * WIDTH :].T
    self_bias[...] = small[0:3]
    self_norm[...] = small[3:5]
    down_bias[...] = small[8:9]
    ffn_norm[...] = small[9:11]
    chunks = up_bias.shape[1] // small.shape[1]
    up_bias[...] = jnp.concatenate([small[11 + chunk : 12 + chunk] for chunk in range(chunks)], axis=1)
    small = own_cross[:, 4 * WIDTH :].T
    cross_bias[...] = small[0:3]
    cross_norm[...] = small[3:5]


smem = pl.BlockSpec(memory_space=pltpu.SMEM)


def fixed(array):
    zeros = (0,) * array.ndim
    return pl.BlockSpec(array.shape, lambda i: zeros, pipeline_mode=pl.Buffered(1))


def rows_of(count, width):
    return pl.BlockSpec((count, width), lambda i: (i, 0))


def total_of(count, width):
    return pl.BlockSpec((count, width), lambda i: (0, 0))


def shape_of(shape, kind):
    return jax.ShapeDtypeStruct(shape, kind)


def flip(count, bit):
    return [(place, place ^ (1 << bit)) for place in range(count)]


def send(parts, axis, bit):
    return lax.ppermute(parts, axis, flip(lax.axis_size(axis), bit))


def local(
    hidden, lengths, task_flags, cotangent, cross_proj, cross_bias, cross_norm, cross_out, self_proj, self_bias,
    self_norm, self_out, ffn_up, up_bias, ffn_down, down_bias, ffn_norm,
):
    _, items, slots, width = hidden.shape
    deep = ffn_up.shape[2]
    rows = items * slots
    streams, places = lax.axis_size("stream"), lax.axis_size("dp")
    bits = places.bit_length() - 1
    steps = items // TILE
    size = TILE * slots
    high = padded(slots)
    groups = items // 2
    item_spec = pl.BlockSpec((slots, TILE, width), lambda i: (0, i, 0))
    row_spec = rows_of(size, width)
    scale_spec = rows_of(size, 1)
    wide_spec = rows_of(size, 3 * width)
    deep_spec = rows_of(size, deep)
    triple_spec = pl.BlockSpec((TILE // 2, 2 * high, 3 * width), lambda i: (i, 0, 0))
    pair_spec = pl.BlockSpec((TILE // 2, 2 * high, width), lambda i: (i, 0, 0))
    probs_spec = pl.BlockSpec((TILE // 2, PAIRS, 4 * high, 2 * high), lambda i: (i, 0, 0, 0))
    any_spec = pl.BlockSpec(memory_space=pl.ANY)
    row_f32, row_bf16 = shape_of((rows, width), f32), shape_of((rows, width), bf16)
    scale_f32 = shape_of((rows, 1), f32)
    wide_bf16, deep_bf16 = shape_of((rows, 3 * width), bf16), shape_of((rows, deep), bf16)
    triple_bf16 = shape_of((groups, 2 * high, 3 * width), bf16)
    pair_f32 = shape_of((groups, 2 * high, width), f32)
    probs_bf16 = shape_of((groups, PAIRS, 4 * high, 2 * high), bf16)
    sum_spec, sum_f32 = total_of(LANES, width), shape_of((LANES, width), f32)
    params = pltpu.CompilerParams(vmem_limit_bytes=vmem_limit)
    unit = 2 * rows * width * width
    stage = pltpu.VMEM((PAIRS, TILE * high, LANES), f32)
    out_stage = pltpu.VMEM((3 * PAIRS, TILE * high, LANES), f32)

    def remote(identity):
        return pltpu.CompilerParams(vmem_limit_bytes=vmem_limit, collective_id=identity, has_side_effects=True)

    def cost(units, count):
        return pl.CostEstimate(flops=units * unit, bytes_accessed=count, transcendentals=0)

    def scratch(*shape, kind=bf16):
        return pltpu.VMEM(shape, kind)

    def semaphores(count):
        return [pltpu.SemaphoreType.DMA((count,))] * 2

    vmem_spec = pl.BlockSpec(memory_space=pltpu.VMEM)

    def held(spec):
        return pl.BlockSpec(spec.block_shape, lambda i: spec.index_map(jnp.minimum(i, steps - 1)))

    def kept_out(*shape):
        zeros = (0,) * len(shape)
        return pl.BlockSpec(shape, lambda i: zeros)

    chunk_bits = (width * places // deep).bit_length() - 1
    share, cross_share = width // places, width // places // streams
    digits = [("dp", bit, 1 << bit) for bit in range(bits)]
    z_digits = [digits[0], digits[2], digits[1]] + digits[3:]
    cross_digits = [digits[0], ("stream", 0, places)] + digits[1:]
    slot_rows = jnp.transpose(hidden[0], (1, 0, 2))
    slot_cotangent = jnp.transpose(cotangent[0], (1, 0, 2))

    (dense, far_dense, triple1, probs1, contexts1, context1, normed1, scale1,
     triple2, probs2, contexts2, context2, normed2, scale2) = pl.pallas_call(
        functools.partial(forward_kernel, slots, steps),
        grid=(steps,),
        in_specs=[smem, any_spec, item_spec] + [any_spec] * 4 + [fixed(w) for w in (cross_bias, cross_norm, self_bias, self_norm)],
        out_specs=[row_spec, row_spec] + [triple_spec, probs_spec, pair_spec, row_spec, row_spec, scale_spec] * 2,
        out_shape=[row_bf16, row_bf16] + [triple_bf16, probs_bf16, pair_f32, row_bf16, row_f32, scale_f32] * 2,
        scratch_shapes=[
            scratch(size, width, kind=f32), scratch(size, width), stage, stage,
            scratch(steps, slots, TILE, width), *[scratch(items, LANES, kind=jnp.int32)] * 2,
            scratch(width, 3 * width), scratch(width, width), scratch(width, 3 * width), scratch(width, width),
            *semaphores(steps + 1), pltpu.SemaphoreType.DMA((4,)),
        ],
        compiler_params=remote(0),
        cost_estimate=cost(12, 40_000_000),
    )(lengths, slot_rows, slot_rows, cross_proj, cross_out, self_proj, self_out, cross_bias, cross_norm, self_bias, self_norm)

    chunks = deep // width
    half, quarter = width // 2, width // 4
    total = 4 * width + LANES
    (output, grad_attended, up_sum, ffn_sum, down_kept, down_sent, up_kept, up_sent) = pl.pallas_call(
        functools.partial(
            ffn_kernel, slots, steps, digits[:chunk_bits], deep // places, z_digits, share, [(axis, bit, 1 << number) for number, (axis, bit, _) in enumerate(digits[chunk_bits:])]),
        grid=(steps + 1,),
        in_specs=[smem, smem, held(row_spec), held(item_spec), any_spec, any_spec]
        + [fixed(w) for w in (self_norm, up_bias, down_bias, ffn_norm)],
        out_specs=[held(item_spec), held(row_spec), total_of(1, deep), total_of(3, width)]
        + [kept_out(chunks * quarter, width)] * 2 + [kept_out(quarter, deep)] * 2,
        out_shape=[shape_of((slots, items, width), bf16), row_f32, shape_of((1, deep), f32), shape_of((3, width), f32)]
        + [shape_of((chunks * quarter, width), bf16)] * 2 + [shape_of((quarter, deep), bf16)] * 2,
        scratch_shapes=[
            scratch(width, deep), scratch(deep, width), scratch(rows, width), scratch(rows, deep), scratch(rows, width),
            scratch(rows, deep), scratch(size, deep, kind=f32), scratch(size, width, kind=f32), scratch(TILE, LANES, kind=jnp.int32),
            *[scratch(chunks, width, width), scratch(chunks, half, width)] * 2,
            pltpu.SemaphoreType.DMA((2,)), *semaphores(chunks), *semaphores(chunks),
        ],
        compiler_params=remote(1),
        cost_estimate=cost(36, 40_000_000),
    )(lengths, task_flags, normed2, slot_cotangent, ffn_up, ffn_down, self_norm, up_bias, down_bias, ffn_norm)

    grad_crossed, down_half, up_half, self_kept, self_sent = pl.pallas_call(
        functools.partial(self_kernel, slots, steps, digits, z_digits, share),
        grid=(steps + 1,),
        in_specs=[held(spec) for spec in (row_spec, row_spec, scale_spec, row_spec, triple_spec, probs_spec, pair_spec)]
        + [fixed(w) for w in (cross_norm, self_norm, ffn_sum, up_sum)] + [any_spec] * 7,
        out_specs=[held(row_spec), kept_out(chunks * quarter, width), kept_out(quarter, deep)] + [kept_out(quarter, total)] * 2,
        out_shape=[row_f32, shape_of((chunks * quarter, width), bf16), shape_of((quarter, deep), bf16)]
        + [shape_of((quarter, total), bf16)] * 2,
        scratch_shapes=[
            stage, out_stage, scratch(width, 3 * width), scratch(width, width), scratch(rows, width),
            scratch(rows, width), scratch(rows, width), scratch(rows, 3 * width), scratch(LANES, width, kind=f32),
            scratch(5, width, width), scratch(5, half, width),
            scratch(chunks * quarter, width), scratch(chunks * quarter, width), scratch(chunks * quarter // 2, width),
            scratch(quarter, deep), scratch(quarter, deep), scratch(quarter // 2, deep),
            pltpu.SemaphoreType.DMA((5,)), *semaphores(5), *semaphores(8),
        ],
        compiler_params=remote(2),
        cost_estimate=cost(18, 40_000_000),
    )(grad_attended, normed2, scale2, normed1, triple2, probs2, contexts2, cross_norm, self_norm, ffn_sum, up_sum,
      self_proj, self_out, context2, down_kept, down_sent, up_kept, up_sent)

    left = width // 16
    finish = bits == 4
    cross_left = left // 2 if finish else left
    box = total - 2 * (4 * width // 3)
    rest_rows = chunks * quarter // 4
    tails = [(left, total), (cross_left, total)]
    grad_hidden, own_down, own_up, own_self, own_cross = pl.pallas_call(
        functools.partial(cross_kernel, slots, steps, cross_digits, cross_share, finish),
        grid=(steps + 1,),
        in_specs=[held(spec) for spec in (row_spec, row_spec, scale_spec, triple_spec, probs_spec, pair_spec)]
        + [fixed(cross_norm)] + [any_spec] * 9,
        out_specs=[any_spec, kept_out(rest_rows, width), kept_out(left, deep)] + [kept_out(*shape) for shape in tails],
        out_shape=[shape_of((slots, items, width), bf16), shape_of((rest_rows, width), f32), shape_of((left, deep), f32)]
        + [shape_of(shape, f32) for shape in tails],
        scratch_shapes=[
            stage, out_stage, scratch(width, 3 * width), scratch(width, width), scratch(2, rows, width),
            scratch(rows, width), scratch(rows, 3 * width), scratch(rows, width, kind=f32), scratch(LANES, width, kind=f32),
            scratch(steps, slots, TILE, width), scratch(steps, slots, TILE, width), scratch(5, width, width), scratch(5, half, width),
            scratch(width, width, kind=f32),
            scratch(2, 2, 2, left, total), scratch(3, 2, 2, left, box), scratch(3, 2, left, box), scratch(3, left, box),
            scratch(32, total), scratch(32, total),
            scratch(4 * rest_rows, width), scratch(2 * rest_rows, width), scratch(rest_rows, width),
            scratch(4 * left, deep), scratch(2 * left, deep), scratch(left, deep),
            scratch(quarter, total), scratch(quarter, total), scratch(quarter // 2, total), scratch(left, total),
            pltpu.SemaphoreType.DMA((8,)), *semaphores(5), *semaphores(steps), *semaphores(14), *semaphores(12),
            pltpu.SemaphoreType.DMA((steps,)),
        ],
        compiler_params=remote(3),
        cost_estimate=cost(18, 40_000_000),
    )(grad_crossed, normed1, scale1, triple1, probs1, contexts1, cross_norm, cross_proj, cross_out, dense, far_dense, context1,
      down_half, up_half, self_kept, self_sent)

    def sum_rest(total, first):
        for bit in range(first, bits):
            half = total.shape[0] // 2
            total = total[:half].astype(f32) + send(total[half:].astype(bf16), "dp", bit).astype(f32)
        return total

    own_down, own_up = sum_rest(own_down, 4), sum_rest(own_up, 4)
    own_self = sum_rest(own_self, 4)
    own_cross = sum_rest(own_cross, 4 if finish else 3)
    share, cross_share = own_self.shape[0], own_cross.shape[0]
    shapes = [
        (slots, items, width), (slots, items, width), own_down.shape, own_up.shape, (share, 3 * width), (share, width), (3, share), (2, share),
        (1, share), (2, share), (1, deep // places), (cross_share, 3 * width), (cross_share, width), (3, cross_share), (2, cross_share),
    ]
    (output, grad_hidden, own_down, own_up, own_self_proj, own_self_out, self_vectors, self_norms, down_vector, ffn_norms, small_up,
     own_cross_proj, own_cross_out, cross_vectors, cross_norms) = pl.pallas_call(
        unpack_kernel,
        in_specs=[vmem_spec] * 6,
        out_specs=[vmem_spec] * len(shapes),
        out_shape=[shape_of(shape, bf16 if at < 2 else f32) for at, shape in enumerate(shapes)],
        compiler_params=params,
        cost_estimate=cost(0, 10_000_000),
    )(output, grad_hidden, own_down, own_up, own_self, own_cross)
    output, grad_hidden = (jnp.transpose(entry, (1, 0, 2))[None] for entry in (output, grad_hidden))
    return (
        output,
        grad_hidden,
        own_cross_proj,
        cross_vectors,
        cross_norms,
        own_cross_out,
        own_self_proj[None],
        self_vectors[None],
        self_norms[None],
        own_self_out[None],
        own_up[None],
        small_up,
        own_down[None],
        down_vector,
        ffn_norms[None],
    )


def solution(mesh):
    in_specs = (
        P("stream", "dp", None, None),
        P("stream", "dp"),
        P("stream", "dp"),
        P("stream", "dp", None, None),
        P(),
        P(),
        P(),
        P(),
        P("stream", None, None),
        P("stream", None, None),
        P("stream", None, None),
        P("stream", None, None),
        P("stream", None, None),
        P("stream", None),
        P("stream", None, None),
        P("stream", None),
        P("stream", None, None),
    )
    out_specs = (
        P("stream", "dp", None, None),
        P("stream", "dp", None, None),
        P(("stream", "dp"), None),
        P(None, ("stream", "dp")),
        P(None, ("stream", "dp")),
        P(("stream", "dp"), None),
        P("stream", "dp", None),
        P("stream", None, "dp"),
        P("stream", None, "dp"),
        P("stream", "dp", None),
        P("stream", "dp", None),
        P("stream", "dp"),
        P("stream", "dp", None),
        P("stream", "dp"),
        P("stream", None, "dp"),
    )
    return jax.shard_map(local, mesh=mesh, in_specs=in_specs, out_specs=out_specs, check_vma=False)
```

```python
import functools

import jax
import jax.numpy as jnp
from jax import lax
from jax.experimental import pallas as pl
from jax.experimental.pallas import tpu as pltpu
from jax.sharding import PartitionSpec as P

HEADS = 12
HEAD_DIM = 64
PAIRS = HEADS // 2
LANES = 2 * HEAD_DIM
TILE = 8
WIDTH = HEADS * HEAD_DIM
MESH = pl.DeviceIdType.MESH

norm_eps = 1e-06
masked_score = -1000000000.0
vmem_limit = 63 * 1024 * 1024

f32 = jnp.float32
bf16 = jnp.bfloat16


def dot(left, right):
    return jnp.dot(left, right, preferred_element_type=f32)


def dot_nt(left, right):
    return lax.dot_general(left, right, (((1,), (1,)), ((), ())), preferred_element_type=f32)


def dot_tn(left, right):
    return lax.dot_general(left, right, (((0,), (0,)), ((), ())), preferred_element_type=f32)


def norm_parts(summed):
    centred = summed - jnp.mean(summed, axis=-1, keepdims=True)
    scaled = lax.rsqrt(jnp.mean(centred * centred, axis=-1, keepdims=True) + norm_eps)
    return centred * scaled, scaled


def norm_backward(upstream, normed, scaled, gain):
    inner = upstream * gain
    return scaled * (
        inner
        - jnp.mean(inner, axis=-1, keepdims=True)
        - normed * jnp.mean(inner * normed, axis=-1, keepdims=True)
    )


def row_sum(rows):
    return jnp.sum(rows, axis=0, keepdims=True)


def gelu_parts(entries):
    size = jnp.abs(entries)
    bell = jnp.exp2(entries * entries * -0.7213475204444817)
    t = 1.0 / (1.0 + size * (0.3275911 * 0.7071067811865476))
    poly = t * (
        0.5 * 0.254829592
        + t
        * (
            0.5 * -0.284496736
            + t * (0.5 * 1.421413741 + t * (0.5 * -1.453152027 + t * (0.5 * 1.061405429)))
        )
    )
    tail = poly * bell
    area = jnp.where(entries >= 0.0, 1.0 - tail, tail)
    return entries * area, area + entries * bell * 0.3989422804014327


def padded(slots):
    return -(-slots // TILE) * TILE


def lane_tiles(ref, at, count):
    return jnp.concatenate([ref[at + tile, :count] for tile in range(PAIRS)], axis=1)


def to_pairs(stage, ref, at, rows, slots):
    count, high = rows.shape[0], padded(slots)
    for tile in range(PAIRS):
        stage[tile, :count] = rows[:, tile * LANES : (tile + 1) * LANES]
    for group in range(TILE // 2):
        for tile in range(PAIRS):
            ref[group, :, at + tile * LANES : at + (tile + 1) * LANES] = pair_rows(stage, tile, group, high).astype(bf16)


def pair_rows(stage, tile, group, high):
    return jnp.concatenate(
        [stage[tile, pl.ds(2 * group + item, high, stride=TILE), :] for item in range(2)], axis=0)


def put_pair(stage, tile, group, rows, high):
    for item in range(2):
        stage[tile, pl.ds(2 * group + item, high, stride=TILE), :] = rows[item * high : (item + 1) * high]


def clear_padding(stage, slots):
    stage[:, slots * TILE :] = jnp.zeros((stage.shape[0], stage.shape[1] - slots * TILE, LANES), f32)


def pair_mask(len_ref, first, high):
    shape = (2 * high, 2 * high)
    row = lax.broadcasted_iota(jnp.int32, shape, 0)
    col = lax.broadcasted_iota(jnp.int32, shape, 1)
    second = row >= high
    low = jnp.where(second, high, 0)
    end = jnp.where(second, high + len_ref[pl.ds(first + 1, 1), : 2 * high], len_ref[pl.ds(first, 1), : 2 * high])
    allowed = (col >= low) & (col < end)
    return jnp.concatenate([allowed, allowed], axis=0)


def first_head(shape):
    return lax.broadcasted_iota(jnp.int32, shape, 1) < HEAD_DIM


def head_stack(rows):
    low, zero = first_head(rows.shape), jnp.zeros_like(rows)
    return jnp.concatenate([jnp.where(low, rows, zero), jnp.where(low, zero, rows)], axis=0)


def head_merge(stacked):
    count = stacked.shape[0] // 2
    return jnp.where(first_head((count, stacked.shape[1])), stacked[:count], stacked[count:])


def batches(size):
    everything = [(group, pair) for group in range(TILE // 2) for pair in range(PAIRS)]
    return [everything[at : at + size] for at in range(0, len(everything), size)]


def head_block(ref, group, part, pair):
    return ref[group, :, part * WIDTH + pair * LANES : part * WIDTH + (pair + 1) * LANES]


def attend(triple_ref, probs_ref, context_ref, stage, len_ref, first_item, slots):
    high = padded(slots)
    ones = jnp.ones((2 * high, LANES), bf16)
    masks = [pair_mask(len_ref, first_item + 2 * group, high) for group in range(TILE // 2)]
    for batch in batches(12):
        scores = [
            jnp.where(
                masks[group],
                dot_nt(head_stack(head_block(triple_ref, group, 0, pair)), head_block(triple_ref, group, 1, pair)),
                masked_score,
            )
            for group, pair in batch
        ]
        largest = [jnp.max(entry, axis=-1, keepdims=True) for entry in scores]
        weights = [jnp.exp(entry - top).astype(bf16) for entry, top in zip(scores, largest)]
        both = [
            dot(entry, jnp.concatenate([head_block(triple_ref, group, 2, pair), ones], axis=1))
            for (group, pair), entry in zip(batch, weights)
        ]
        for (group, pair), entry, sums in zip(batch, weights, both):
            inverse = 1.0 / sums[:, LANES:]
            probs_ref[group, pair] = (entry.astype(f32) * inverse[:, : 2 * high]).astype(bf16)
            context = head_merge(sums[:, :LANES] * inverse)
            context_ref[group, :, pair * LANES : (pair + 1) * LANES] = context
            put_pair(stage, pair, group, context, high)


def attend_back(triple_ref, probs_ref, context_ref, stage, out_stage, slots):
    high = padded(slots)
    ones = jnp.ones((2 * high, LANES), bf16)
    low = first_head((2 * high, LANES))
    for batch in batches(6):
        stacks, grad_probs = [], []
        for group, pair in batch:
            grads = pair_rows(stage, pair, group, high)
            delta = -grads * context_ref[group, :, pair * LANES : (pair + 1) * LANES]
            upper = delta.astype(bf16)
            lower = pltpu.roll(delta - upper.astype(f32), HEAD_DIM, 1).astype(bf16)
            deltas = jnp.concatenate([jnp.where(low, upper, lower), jnp.where(low, lower, upper)], axis=0)
            stacks.append(head_stack(grads.astype(bf16)))
            values = head_block(triple_ref, group, 2, pair)
            grad_probs.append(
                dot_nt(jnp.concatenate([stacks[-1], deltas], axis=1), jnp.concatenate([values, ones], axis=1)))
        grad_scores = [
            (probs_ref[group, pair].astype(f32) * entry).astype(bf16) for (group, pair), entry in zip(batch, grad_probs)]
        grad_queries = [dot(entry, head_block(triple_ref, group, 1, pair)) for (group, pair), entry in zip(batch, grad_scores)]
        grad_values = [dot_tn(probs_ref[group, pair], entry) for (group, pair), entry in zip(batch, stacks)]
        grad_keys = [
            dot_tn(entry, head_stack(head_block(triple_ref, group, 0, pair))) for (group, pair), entry in zip(batch, grad_scores)]
        for at, (group, pair) in enumerate(batch):
            put_pair(out_stage, pair, group, head_merge(grad_queries[at]) * HEAD_DIM**-0.5, high)
            put_pair(out_stage, PAIRS + pair, group, grad_keys[at], high)
            put_pair(out_stage, 2 * PAIRS + pair, group, grad_values[at], high)


def across(axis, bit):
    place, weight = lax.axis_index(axis), 1 << bit
    return {axis: place + weight - 2 * weight * ((place // weight) % 2)}


def own_bit(axis, bit):
    return (lax.axis_index(axis) // (1 << bit)) % 2


def greet(partners):
    barrier = pltpu.get_barrier_semaphore()
    for partner in partners:
        pl.semaphore_signal(barrier, inc=1, device_id=partner, device_id_type=MESH)
    pl.semaphore_wait(barrier, len(partners))


def remote_copy(source, target, sems, at, partner):
    return pltpu.make_async_remote_copy(
        src_ref=source, dst_ref=target, send_sem=sems[0].at[at], recv_sem=sems[1].at[at],
        device_id=partner, device_id_type=MESH)


def row_slices(slots):
    step = 6 if slots % 6 == 0 else slots
    return [slice(at * TILE, (at + step) * TILE) for at in range(0, slots, step)]


def fold(rows):
    return jnp.sum(rows.reshape(rows.shape[0] // TILE, TILE, rows.shape[1]), axis=0)


def norm_rows(wide, normed_ref, scale_ref, gain, shift, low, slots):
    for rows in row_slices(slots):
        normed, scale = norm_parts(wide[rows])
        normed_ref[rows] = normed
        scale_ref[rows] = scale
        result = normed * gain + shift
        wide[rows] = result
        if low is not None:
            low[rows] = result.astype(bf16)


def norm_back_rows(upstream_ref, normed_ref, scale_ref, gain, grad_ref, low_ref, vec_sum, slots):
    sums = [0.0, 0.0, 0.0]
    for rows in row_slices(slots):
        upstream, normed = upstream_ref[rows], normed_ref[rows]
        grad = norm_backward(upstream, normed, scale_ref[rows], gain)
        low = grad.astype(bf16)
        grad_ref[rows] = grad
        low_ref[rows] = low
        sums = [total + fold(part) for total, part in zip(sums, (low.astype(f32), upstream * normed, upstream))]
    for at, total in enumerate(sums):
        vec_sum[2 + at : 3 + at] += row_sum(total)


def forward_kernel(
    slots, steps,
    lengths, whole, hidden, cross_proj_at, cross_out_at, self_proj_at, self_out_at, cross_bias, cross_norm, self_bias, self_norm,
    dense, far_dense, triple1, probs1, contexts1, context1, normed1, scale1,
    triple2, probs2, contexts2, context2, normed2, scale2,
    wide, low, stage, context_stage, far, lens, far_lens, cross_proj, cross_out, self_proj, self_out, send_sem, recv_sem, load_sem,
):
    count = slots * TILE
    step = pl.program_id(0)
    partner = across("stream", 0)
    sources = [cross_proj_at, cross_out_at, self_proj_at.at[0], self_out_at.at[0]]
    loads = [
        pltpu.make_async_copy(source, target, load_sem.at[at])
        for at, (source, target) in enumerate(zip(sources, [cross_proj, cross_out, self_proj, self_out]))
    ]

    def travel(part):
        if part == steps:
            source, target = lens, far_lens
        else:
            source, target = whole.at[:, pl.ds(part * TILE, TILE)], far.at[part]
        return remote_copy(source, target, (send_sem, recv_sem), part, partner)

    @pl.when(step == 0)
    def _():
        loads[0].start()
        for item in range(lens.shape[0]):
            lens[item : item + 1] = jnp.full((1, LANES), lengths[0, item], jnp.int32)
        greet([partner])
        travel(steps).start()
        for part in range(steps):
            travel(part).start()
        for load in loads[1:]:
            load.start()
        clear_padding(stage, slots)
        loads[0].wait()

    rows = hidden[...].astype(f32).reshape(count, WIDTH)
    wide[...] = rows
    dense[...] = rows.astype(bf16)
    queries = (dot(dense[...], cross_proj[:, :WIDTH]) + cross_bias[0:1]).astype(bf16).astype(f32)
    to_pairs(stage, triple1, 0, queries * HEAD_DIM**-0.5, slots)

    @pl.when(step == 0)
    def _():
        travel(steps).wait()
        for load in loads[1:]:
            load.wait()

    for part in range(steps):

        @pl.when(step == part)
        def _():
            travel(part).wait()

    far_dense[...] = far[step].astype(f32).reshape(count, WIDTH).astype(bf16)
    to_pairs(stage, triple1, WIDTH, dot(far_dense[...], cross_proj[:, WIDTH : 2 * WIDTH]), slots)
    to_pairs(stage, triple1, 2 * WIDTH, dot(far_dense[...], cross_proj[:, 2 * WIDTH :]) + cross_bias[1:2], slots)
    attend(triple1, probs1, contexts1, context_stage, far_lens, step * TILE, slots)
    context1[...] = lane_tiles(context_stage, 0, count).astype(bf16)
    wide[...] += dot(context1[...], cross_out[...]) + cross_bias[2:3]
    norm_rows(wide, normed1, scale1, cross_norm[0:1], cross_norm[1:2], low, slots)
    queries = (dot(low[...], self_proj[:, :WIDTH]) + self_bias[0]).astype(bf16).astype(f32)
    to_pairs(stage, triple2, 0, queries * HEAD_DIM**-0.5, slots)
    to_pairs(stage, triple2, WIDTH, dot(low[...], self_proj[:, WIDTH : 2 * WIDTH]), slots)
    to_pairs(stage, triple2, 2 * WIDTH, dot(low[...], self_proj[:, 2 * WIDTH :]) + self_bias[1], slots)
    attend(triple2, probs2, contexts2, context_stage, lens, step * TILE, slots)
    context2[...] = lane_tiles(context_stage, 0, count).astype(bf16)
    wide[...] += dot(context2[...], self_out[...]) + self_bias[2]
    for rows in row_slices(slots):
        normed, scale = norm_parts(wide[rows])
        normed2[rows] = normed
        scale2[rows] = scale


def order_rows(digits, share):
    shape = (WIDTH, WIDTH)
    row, col = (lax.broadcasted_iota(jnp.int32, shape, dim) for dim in range(2))
    block, spot = col // share, 0
    for axis, bit, weight in digits:
        mine, other = own_bit(axis, bit), (block // weight) % 2
        spot = 2 * spot + mine + other - 2 * mine * other
    return jnp.where(row == spot * share + col % share, 1.0, 0.0).astype(bf16)


def own_first(digits, block):
    spot = 0
    for axis, bit, weight in digits:
        mine, other = own_bit(axis, bit), (block // weight) % 2
        spot = 2 * spot + mine + other - 2 * mine * other
    return spot


class Products:
    def __init__(self, share, both, inbox, sems, wide=None, order=None):
        self.share, self.both, self.inbox, self.sems, self.wide, self.order = share, both, inbox, sems, wide, order
        self.half = WIDTH // 2
        self.small = self.share % (TILE if wide is not None else 2 * TILE) != 0

    def travel(self, at):
        return remote_copy(self.both.at[at, pl.ds(self.half, self.half)], self.inbox.at[at], self.sems, at, across("dp", 0))

    def put(self, at, product, digits):
        columns = slice(0, product.shape[1])
        if self.small:
            self.both[at, :, columns] = dot(order_rows(digits, self.share), product.astype(bf16)).astype(bf16)
        elif self.wide is not None:
            for block in range(WIDTH // self.share):
                spot = pl.multiple_of(own_first(digits, block) * self.share, TILE)
                self.wide[pl.ds(spot, self.share), columns] = product[block * self.share : (block + 1) * self.share]
            self.both[at, :, columns] = self.wide[:, columns].astype(bf16)
        else:
            for block in range(WIDTH // self.share):
                spot = pl.multiple_of(own_first(digits, block) * self.share, 2 * TILE)
                self.both[at, pl.ds(spot, self.share), columns] = product[block * self.share : (block + 1) * self.share].astype(bf16)
        self.travel(at).start()

    def send(self, at, left, right, digits):
        self.put(at, dot_tn(left, right), digits)

    def send_sums(self, at, sums, digits):
        self.put(at, sums.T, digits)

    def keep(self, at, wide=WIDTH):
        self.travel(at).wait()
        return self.both[at, : self.half, :wide].astype(f32) + self.inbox[at, :, :wide].astype(f32)


class Halving:
    def __init__(self, now, boxes, sems, base, partners, first=None):
        self.now, self.boxes, self.sems, self.base, self.partners, self.first = now, boxes, sems, base, partners, first

    def travel(self, stage):
        box = self.boxes[stage]
        source = self.first
        if stage > 0 or source is None:
            source = self.now.at[pl.ds(box.shape[0], box.shape[0])]
        return remote_copy(source, box, self.sems, self.base + stage, self.partners[stage])

    def start(self, stage):
        self.travel(stage).start()

    def total(self, stage):
        self.travel(stage).wait()
        box = self.boxes[stage]
        return self.now[: box.shape[0]].astype(f32) + box[...].astype(f32)

    def finish(self, stage):
        self.now[: self.boxes[stage].shape[0]] = self.total(stage).astype(bf16)


def ffn_rows(
    slots, step, live, normed2, cotangent, self_norm, ffn_up, up_bias, ffn_down, down_bias, ffn_norm, down_load,
    output, grad_attended, attended_low, activated, grad_last_low, grad_expanded, up_sum, vec_sum, slope, wide,
):
    count = slots * TILE
    here = pl.ds(pl.multiple_of(step * count, count), count)
    chunks = ffn_up.shape[1] // WIDTH
    attended = normed2[...] * self_norm[0, 0:1] + self_norm[0, 1:2]
    attended_low[here] = attended.astype(bf16)
    wide[...] = attended + down_bias[...]
    parts = [slice(chunk * WIDTH, (chunk + 1) * WIDTH) for chunk in range(chunks)]

    def rise(part):
        return dot(attended_low[here], ffn_up[:, part]) + up_bias[:, part]

    entries = rise(parts[0])
    for number, part in enumerate(parts):
        later = rise(parts[number + 1]) if number + 1 < chunks else None
        active, steep = gelu_parts(entries)
        activated[here, part] = active.astype(bf16)
        slope[:, part] = steep
        if number == 0:

            @pl.when(step == 0)
            def _():
                down_load.wait()

        wide[...] += dot(activated[here, part], ffn_down[part, :])
        entries = later
    each = slots // len(row_slices(slots))
    sums = [0.0, 0.0, 0.0]
    alive = jnp.concatenate([live[...]] * PAIRS, axis=1)
    for number, rows in enumerate(row_slices(slots)):
        spots = slice(number * each, (number + 1) * each)
        shape = (each, TILE, WIDTH)
        normed, scale = norm_parts(wide[rows])
        output[spots] = (normed * ffn_norm[0, 0:1] + ffn_norm[0, 1:2]).reshape(shape).astype(bf16)
        slot = lax.broadcasted_iota(jnp.int32, shape, 0) + number * each
        upstream = jnp.where(slot < alive[None], cotangent[spots].astype(f32), 0.0).reshape(each * TILE, WIDTH)
        grad = norm_backward(upstream, normed, scale, ffn_norm[0, 0:1])
        low = grad.astype(bf16)
        wide[rows] = grad
        grad_last_low[pl.ds(pl.multiple_of(step * count + number * each * TILE, each * TILE), each * TILE)] = low
        sums = [total + fold(part) for total, part in zip(sums, (low.astype(f32), upstream * normed, upstream))]
    for at, total in enumerate(sums):
        vec_sum[at : at + 1] += row_sum(total)
    grad_low = grad_last_low[here]
    total = wide[...]
    for part in parts:
        grad_up = (dot_nt(grad_low, ffn_down[part, :]) * slope[:, part]).astype(bf16)
        grad_expanded[here, part] = grad_up
        up_sum[:, part] += row_sum(grad_up.astype(f32))
        total = total + dot_nt(grad_up, ffn_up[:, part])
    grad_attended[...] = total


def ffn_kernel(
    slots, steps, down_digits, down_share, up_digits, up_share, chunk_digits,
    lengths, flags, normed2, cotangent, ffn_up_at, ffn_down_at, self_norm, up_bias, down_bias, ffn_norm,
    output, grad_attended, up_sum, vec_sum, down_kept, down_sent, up_kept, up_sent,
    ffn_up, ffn_down, attended_low, activated, grad_last_low, grad_expanded, slope, wide, live,
    down_both, down_in, up_both, up_in, load_sem, down_send, down_recv, up_send, up_recv,
):
    step = pl.program_id(0)
    chunks = ffn_up.shape[1] // WIDTH
    loads = [
        pltpu.make_async_copy(ffn_up_at.at[0], ffn_up, load_sem.at[0]),
        pltpu.make_async_copy(ffn_down_at.at[0], ffn_down, load_sem.at[1]),
    ]

    @pl.when(step == 0)
    def _():
        for load in loads:
            load.start()
        greet([across("dp", 0)])
        up_sum[...] = jnp.zeros_like(up_sum)
        vec_sum[...] = jnp.zeros_like(vec_sum)
        loads[0].wait()

    @pl.when(step < steps)
    def _():
        for item in range(TILE):
            count = jnp.where(flags[0, step * TILE + item] > 0, lengths[0, step * TILE + item], 0)
            live[item : item + 1] = jnp.full((1, LANES), count, jnp.int32)
        ffn_rows(
            slots, step, live, normed2, cotangent, self_norm, ffn_up, up_bias, ffn_down, down_bias, ffn_norm, loads[1],
            output, grad_attended, attended_low, activated, grad_last_low, grad_expanded, up_sum, vec_sum, slope, wide)

    @pl.when(step == steps)
    def _():
        quarter = WIDTH // 4
        down = Products(down_share, down_both, down_in, (down_send, down_recv))
        up = Products(up_share, up_both, up_in, (up_send, up_recv))
        inner = quarter // down_share

        def keep_down(chunk):
            product = down.keep(chunk).astype(bf16)
            place = own_first(chunk_digits, chunk)
            for piece in range(inner):
                spot = pl.ds(pl.multiple_of((piece * chunks + place) * down_share, 16), down_share)
                from_own = slice(piece * down_share, (piece + 1) * down_share)
                from_other = slice(quarter + piece * down_share, quarter + (piece + 1) * down_share)
                down_kept[spot, :] = product[from_own]
                down_sent[spot, :] = product[from_other]

        def keep_up(chunk):
            product = up.keep(chunk).astype(bf16)
            at = slice(chunk * WIDTH, (chunk + 1) * WIDTH)
            up_kept[:, at] = product[:quarter]
            up_sent[:, at] = product[quarter:]

        for chunk in range(chunks):
            down.send(chunk, activated[:, chunk * WIDTH : (chunk + 1) * WIDTH], grad_last_low[...], down_digits)
            if chunk > 1:
                keep_down(chunk - 2)
        for chunk in range(chunks):
            up.send(chunk, attended_low[...], grad_expanded[:, chunk * WIDTH : (chunk + 1) * WIDTH], up_digits)
            if chunk < 2:
                keep_down(chunks - 2 + chunk)
            else:
                keep_up(chunk - 2)
        keep_up(chunks - 2)
        keep_up(chunks - 1)


def context_back(low, out, triple, probs, contexts, grad_triple, here, vec_sum, stage, out_stage, slots):
    count = slots * TILE
    grads = dot_nt(low, out).astype(bf16).astype(f32)
    for tile in range(PAIRS):
        stage[tile, :count] = grads[:, tile * LANES : (tile + 1) * LANES]
    attend_back(triple, probs, contexts, stage, out_stage, slots)
    for part in range(3):
        rows = lane_tiles(out_stage, part * PAIRS, count).astype(bf16)
        grad_triple[here, part * WIDTH : (part + 1) * WIDTH] = rows
        if part != 1:
            vec_sum[part // 2 : part // 2 + 1] += row_sum(rows.astype(f32))


def self_kernel(
    slots, steps, digits, z_digits, share,
    grad_attended, normed2, scale2, normed1, triple2, probs2, contexts2,
    cross_norm, self_norm, ffn_sum, up_sum, self_proj_at, self_out_at, context_at,
    down_kept, down_sent, up_kept, up_sent,
    grad_crossed, down_half, up_half, self_kept, self_sent,
    stage, out_stage, self_proj, self_out, context, crossed_low, grad_mid_low, grad_triple, vec_sum,
    both, inbox,
    down_now, down_box1, down_box2, up_now, up_box1, up_box2, load_sem, send_sem, recv_sem, sum_send, sum_recv,
):
    step = pl.program_id(0)
    count = slots * TILE
    here = pl.ds(pl.multiple_of(step * count, count), count)
    near, next_one = across("dp", 1), across("dp", 2)
    sums = (sum_send, sum_recv)
    early, late = [], []
    for number, (now, boxes, route, sent) in enumerate((
        (down_now, (down_box1, down_box2), [near, next_one], down_sent), (up_now, (up_box1, up_box2), [next_one, near], up_sent),
    )):
        cut = now.shape[1] // 2
        for place, group in enumerate((early, late)):
            columns = pl.ds(place * cut, cut)
            group.append(Halving(
                now.at[:, columns], [box.at[:, columns] for box in boxes], sums, 4 * number + 2 * place, route, sent.at[:, columns]))
    pairs = [
        (self_out_at.at[0], self_out), (self_proj_at.at[0], self_proj), (down_kept, down_now), (up_kept, up_now),
        (context_at, context),
    ]
    loads = [pltpu.make_async_copy(source, target, load_sem.at[at]) for at, (source, target) in enumerate(pairs)]

    @pl.when(step == 0)
    def _():
        loads[0].start()
        greet([across("dp", 0), near, next_one])
        for part in early:
            part.start(0)
        for load in loads[1:]:
            load.start()
        vec_sum[...] = jnp.zeros_like(vec_sum)
        clear_padding(stage, slots)
        loads[0].wait()
        loads[1].wait()

    @pl.when(step < steps)
    def _():
        norm_back_rows(grad_attended, normed2, scale2, self_norm[0, 0:1], grad_crossed, grad_mid_low.at[here], vec_sum, slots)
        crossed_low[here] = (normed1[...] * cross_norm[0:1] + cross_norm[1:2]).astype(bf16)
        context_back(grad_mid_low[here], self_out[...], triple2, probs2, contexts2, grad_triple, here, vec_sum, stage, out_stage, slots)
        grad_crossed[...] += dot_nt(grad_triple[here], self_proj[...])

    @pl.when(step == 0)
    def _():
        for part in late:
            part.start(0)

    @pl.when(step == steps - 2)
    def _():
        loads[2].wait()
        loads[3].wait()
        for part in early:
            part.finish(0)
            part.start(1)

    @pl.when(step == steps)
    def _():
        loads[4].wait()
        vec_sum[8:11] = ffn_sum[...]
        chunks = up_sum.shape[1] // WIDTH
        for chunk in range(chunks):
            vec_sum[16 + chunk : 17 + chunk] = up_sum[:, chunk * WIDTH : (chunk + 1) * WIDTH]
        quarter = WIDTH // 4
        products = Products(share, both, inbox, (send_sem, recv_sem))
        orders = [digits, digits, digits, z_digits, z_digits]

        def keep(at, wide=WIDTH):
            product = products.keep(at, wide).astype(bf16)
            columns = slice(at * WIDTH, at * WIDTH + wide)
            self_kept[:, columns] = product[:quarter]
            self_sent[:, columns] = product[quarter:]

        for part in range(3):
            products.send(part, crossed_low[...], grad_triple[:, part * WIDTH : (part + 1) * WIDTH], orders[part])
            if part > 0:
                keep(part - 1)
        products.send(3, context[...], grad_mid_low[...], orders[3])
        keep(2)
        turned = vec_sum[...].T
        lane = lax.broadcasted_iota(jnp.int32, (share, LANES), 1)
        wide = [jnp.broadcast_to(turned[:, 16 + chunk : 17 + chunk], (WIDTH, LANES)) for chunk in range(chunks)]
        pieces = []
        for place in range(WIDTH // share):
            piece = turned[place * share : (place + 1) * share]
            for column in range(chunks):
                source = (place * chunks + column) * share
                rows = wide[source // WIDTH][source % WIDTH : source % WIDTH + share]
                piece = jnp.where(lane == 11 + column, rows, piece)
            pieces.append(piece)
        products.put(4, jnp.concatenate(pieces, axis=0), orders[4])
        keep(3)
        keep(4, LANES)
        for part in late:
            part.finish(0)
        for part in early:
            part.finish(1)
        down_half[...] = down_now[...]
        up_half[...] = up_now[...]


def cross_kernel(
    slots, steps, digits, share, finish,
    grad_crossed, normed1, scale1, triple1, probs1, contexts1,
    cross_norm, cross_proj_at, cross_out_at, dense_at, far_at, context_at,
    down_at, up_at, self_kept, self_sent,
    grad_hidden, own_down, own_up, self_result, cross_result,
    stage, out_stage, cross_proj, cross_out, lefts, grad_cross_low, grad_triple, grad_own, vec_sum,
    dx_out, dx_in, both, inbox, wide, total, box1, box2, box3, last_out, last_in,
    down_now, down_box1, down_box2, up_now, up_box1, up_box2, self_now, self_box1, self_box2, self_box3,
    load_sem, send_sem, recv_sem, dx_send, dx_recv, sum_send, sum_recv, part_send, part_recv, out_sem,
):
    step = pl.program_id(0)
    count = slots * TILE
    here = pl.ds(pl.multiple_of(step * count, count), count)
    links = [across("stream", 0), across("dp", 1), across("dp", 2)]
    sums = (sum_send, sum_recv)
    last = across("dp", 3)
    early, late = [], []
    for number, (now, boxes, route) in enumerate((
        (down_now, (down_box1, down_box2), [links[2], last]), (up_now, (up_box1, up_box2), [links[1], last]),
    )):
        cut = now.shape[1] // 2
        high = now.shape[0] // 2
        early.append(Halving(
            now.at[pl.ds(0, high), pl.ds(0, cut)], [boxes[1].at[:, pl.ds(0, cut)]], sums, 8 + number, route[1:]))
        columns = pl.ds(cut, cut)
        late.append(Halving(now.at[:, columns], [box.at[:, columns] for box in boxes], sums, 10 + 2 * number, route))
    middle = 3 * WIDTH
    own = []
    for number, (columns, route) in enumerate((
        (pl.ds(0, middle), [links[1], links[2], last]), (pl.ds(middle, self_now.shape[1] - middle), [links[2], links[1], last]),
    )):
        boxes = [box.at[:, columns] for box in (self_box1, self_box2, self_box3)]
        own.append(Halving(self_now.at[:, columns], boxes, sums, 3 * number, route, self_sent.at[:, columns]))
    pairs = [
        (cross_out_at, cross_out), (cross_proj_at, cross_proj), (down_at, down_now), (up_at, up_now), (self_kept, self_now),
        (dense_at, lefts.at[0]), (far_at, lefts.at[1]), (context_at, lefts.at[0]),
    ]
    loads = [pltpu.make_async_copy(source, target, load_sem.at[at]) for at, (source, target) in enumerate(pairs)]

    def travel(part):
        return remote_copy(dx_out.at[part], dx_in.at[part], (dx_send, dx_recv), part, links[0])

    @pl.when(step == 0)
    def _():
        for at in (0, 2, 3, 1, 4):
            loads[at].start()
        greet(links + [last, across("dp", 0)])
        loads[2].wait()
        loads[3].wait()
        for part in early + late + own:
            part.start(0)
        for at in (5, 6):
            loads[at].start()
        vec_sum[...] = jnp.zeros_like(vec_sum)
        clear_padding(stage, slots)
        loads[0].wait()
        loads[1].wait()

    @pl.when(step < steps)
    def _():
        norm_back_rows(grad_crossed, normed1, scale1, cross_norm[0:1], grad_own.at[here], grad_cross_low.at[here], vec_sum, slots)
        context_back(grad_cross_low[here], cross_out[...], triple1, probs1, contexts1, grad_triple, here, vec_sum, stage, out_stage, slots)
        dx_out[step] = dot_nt(grad_triple[here, WIDTH:], cross_proj[:, WIDTH:]).reshape(slots, TILE, WIDTH).astype(bf16)
        travel(step).start()
        grad_own[here] += dot_nt(grad_triple[here, :WIDTH], cross_proj[:, :WIDTH])

    @pl.when(step == steps - 2)
    def _():
        for part in late:
            part.finish(0)
            part.start(1)

    @pl.when(step == steps)
    def _():
        for at in range(4, len(loads) - 1):
            loads[at].wait()
        for part in own:
            part.finish(0)
            part.start(1)
        products = Products(share, both, inbox, (send_sem, recv_sem), wide)
        cut = 3 * WIDTH // 2
        bounds = [(0, cut), (cut, 2 * cut), (2 * cut, total.shape[-1])]
        routes = [(0, 1, 2), (1, 0, 2), (2, 0, 1)]
        boxes = [box1, box2, box3]

        def view(part, stage, sent):
            spot = [slice(None)] * 3
            for axis in routes[part][:stage]:
                spot[axis] = 0
            spot[routes[part][stage]] = sent
            return tuple(spot) + (slice(None), slice(*bounds[part]))

        def box_view(part, stage):
            wide = bounds[part][1] - bounds[part][0]
            return (part,) + (slice(None),) * (3 - stage) + (slice(0, wide),)

        def hop(part, stage):
            return remote_copy(
                total.at[view(part, stage, 1)], boxes[stage].at[box_view(part, stage)], (part_send, part_recv),
                3 * part + stage, links[routes[part][stage]])

        def keep(at, wide=WIDTH):
            product = products.keep(at, wide)
            total[:, :, :, :, at * WIDTH : at * WIDTH + wide] = product.reshape(2, 2, 2, product.shape[0] // 8, wide).astype(bf16)

        products.send(0, lefts[0], grad_triple[:, :WIDTH], digits)
        loads[7].start()
        products.send(1, lefts[1], grad_triple[:, WIDTH : 2 * WIDTH], digits)
        keep(0)
        products.send(2, lefts[1], grad_triple[:, 2 * WIDTH :], digits)
        keep(1)
        hop(0, 0).start()
        loads[7].wait()
        products.send(3, lefts[0], grad_cross_low[...], digits)
        keep(2)
        hop(1, 0).start()
        products.send_sums(4, vec_sum[...], digits)
        keep(3)
        keep(4, LANES)
        hop(2, 0).start()
        for part in own:
            part.finish(1)
            part.start(2)
        def leave(part):
            return pltpu.make_async_copy(dx_out.at[part], grad_hidden.at[:, pl.ds(part * TILE, TILE)], out_sem.at[part])

        def write(part):
            travel(part).wait()
            value = grad_own[part * count : (part + 1) * count].reshape(slots, TILE, WIDTH) + dx_in[part].astype(f32)
            dx_out[part] = value.astype(bf16)
            leave(part).start()

        for part in range(steps):
            write(part)
        last_rows = total.shape[3] // 2

        def last_hop(part):
            columns = pl.ds(bounds[part][0], bounds[part][1] - bounds[part][0])
            return remote_copy(last_out.at[:, columns], last_in.at[:, columns], (part_send, part_recv), 9 + part, last)

        kept = []
        for stage_at in range(3):
            for part in range(3):
                hop(part, stage_at).wait()
                spot = view(part, stage_at, 0)
                summed = total[spot].astype(f32) + boxes[stage_at][box_view(part, stage_at)].astype(f32)
                if stage_at < 2:
                    total[spot] = summed.astype(bf16)
                    hop(part, stage_at + 1).start()
                elif not finish:
                    cross_result[:, slice(*bounds[part])] = summed
                else:
                    kept.append(summed[:last_rows])
                    gap = jnp.zeros((last_out.shape[0] - last_rows, summed.shape[1]), f32)
                    last_out[:, slice(*bounds[part])] = jnp.concatenate([summed[last_rows:], gap], axis=0).astype(bf16)
                    last_hop(part).start()
        for first, second, result in zip(early, late, (own_down, own_up)):
            cut = result.shape[1] // 2
            result[:, :cut] = first.total(0)
            result[:, cut:] = second.total(1)
        self_result[...] = jnp.concatenate([part.total(2) for part in own], axis=1)
        if finish:
            for part in range(3):
                last_hop(part).wait()
            cross_result[...] = jnp.concatenate(kept, axis=1) + last_in[...].astype(f32)[:last_rows]
        for part in range(steps):
            leave(part).wait()


def unpack_kernel(
    output, grad_hidden, own_down, own_up, own_self, own_cross,
    output_to, grad_hidden_to, own_down_to, own_up_to, self_proj, self_out, self_bias, self_norm, down_bias, ffn_norm, up_bias,
    cross_proj, cross_out, cross_bias, cross_norm,
):
    for source, target in zip((output, grad_hidden, own_down, own_up), (output_to, grad_hidden_to, own_down_to, own_up_to)):
        target[...] = source[...]
    for source, wide, narrow in ((own_self, self_proj, self_out), (own_cross, cross_proj, cross_out)):
        wide[...] = source[:, : 3 * WIDTH]
        narrow[...] = source[:, 3 * WIDTH : 4 * WIDTH]
    small = own_self[:, 4 * WIDTH :].T
    for at in range(3):
        self_bias[at] = small[at : at + 1]
    self_norm[...] = small[3:5]
    down_bias[...] = small[8:9]
    ffn_norm[...] = small[9:11]
    chunks = up_bias.shape[1] // small.shape[1]
    up_bias[...] = jnp.concatenate([small[11 + chunk : 12 + chunk] for chunk in range(chunks)], axis=1)
    small = own_cross[:, 4 * WIDTH :].T
    cross_bias[...] = small[0:3]
    cross_norm[...] = small[3:5]


smem = pl.BlockSpec(memory_space=pltpu.SMEM)


def fixed(array):
    zeros = (0,) * array.ndim
    return pl.BlockSpec(array.shape, lambda i: zeros, pipeline_mode=pl.Buffered(1))


def rows_of(count, width):
    return pl.BlockSpec((count, width), lambda i: (i, 0))


def total_of(count, width):
    return pl.BlockSpec((count, width), lambda i: (0, 0))


def shape_of(shape, kind):
    return jax.ShapeDtypeStruct(shape, kind)


def flip(count, bit):
    return [(place, place ^ (1 << bit)) for place in range(count)]


def send(parts, axis, bit):
    return lax.ppermute(parts, axis, flip(lax.axis_size(axis), bit))


def local(
    hidden, lengths, task_flags, cotangent, cross_proj, cross_bias, cross_norm, cross_out, self_proj, self_bias,
    self_norm, self_out, ffn_up, up_bias, ffn_down, down_bias, ffn_norm,
):
    _, items, slots, width = hidden.shape
    deep = ffn_up.shape[2]
    rows = items * slots
    streams, places = lax.axis_size("stream"), lax.axis_size("dp")
    bits = places.bit_length() - 1
    steps = items // TILE
    size = TILE * slots
    high = padded(slots)
    groups = items // 2
    item_spec = pl.BlockSpec((slots, TILE, width), lambda i: (0, i, 0))
    row_spec = rows_of(size, width)
    scale_spec = rows_of(size, 1)
    wide_spec = rows_of(size, 3 * width)
    deep_spec = rows_of(size, deep)
    triple_spec = pl.BlockSpec((TILE // 2, 2 * high, 3 * width), lambda i: (i, 0, 0))
    pair_spec = pl.BlockSpec((TILE // 2, 2 * high, width), lambda i: (i, 0, 0))
    probs_spec = pl.BlockSpec((TILE // 2, PAIRS, 4 * high, 2 * high), lambda i: (i, 0, 0, 0))
    any_spec = pl.BlockSpec(memory_space=pl.ANY)
    row_f32, row_bf16 = shape_of((rows, width), f32), shape_of((rows, width), bf16)
    scale_f32 = shape_of((rows, 1), f32)
    wide_bf16, deep_bf16 = shape_of((rows, 3 * width), bf16), shape_of((rows, deep), bf16)
    triple_bf16 = shape_of((groups, 2 * high, 3 * width), bf16)
    pair_f32 = shape_of((groups, 2 * high, width), f32)
    probs_bf16 = shape_of((groups, PAIRS, 4 * high, 2 * high), bf16)
    sum_spec, sum_f32 = total_of(LANES, width), shape_of((LANES, width), f32)
    params = pltpu.CompilerParams(vmem_limit_bytes=vmem_limit)
    unit = 2 * rows * width * width
    stage = pltpu.VMEM((PAIRS, TILE * high, LANES), f32)
    out_stage = pltpu.VMEM((3 * PAIRS, TILE * high, LANES), f32)

    def remote(identity):
        return pltpu.CompilerParams(vmem_limit_bytes=vmem_limit, collective_id=identity, has_side_effects=True)

    def cost(units, count):
        return pl.CostEstimate(flops=units * unit, bytes_accessed=count, transcendentals=0)

    def scratch(*shape, kind=bf16):
        return pltpu.VMEM(shape, kind)

    def semaphores(count):
        return [pltpu.SemaphoreType.DMA((count,))] * 2

    vmem_spec = pl.BlockSpec(memory_space=pltpu.VMEM)

    def held(spec):
        return pl.BlockSpec(spec.block_shape, lambda i: spec.index_map(jnp.minimum(i, steps - 1)))

    def kept_out(*shape):
        zeros = (0,) * len(shape)
        return pl.BlockSpec(shape, lambda i: zeros)

    chunk_bits = (width * places // deep).bit_length() - 1
    share, cross_share = width // places, width // places // streams
    digits = [("dp", bit, 1 << bit) for bit in range(bits)]
    z_digits = [digits[0], digits[2], digits[1]] + digits[3:]
    cross_digits = [digits[0], ("stream", 0, places)] + digits[1:]
    bias_rows = jnp.transpose(self_bias, (1, 0, 2))
    slot_rows = jnp.transpose(hidden[0], (1, 0, 2))
    slot_cotangent = jnp.transpose(cotangent[0], (1, 0, 2))

    (dense, far_dense, triple1, probs1, contexts1, context1, normed1, scale1,
     triple2, probs2, contexts2, context2, normed2, scale2) = pl.pallas_call(
        functools.partial(forward_kernel, slots, steps),
        grid=(steps,),
        in_specs=[smem, any_spec, item_spec] + [any_spec] * 4 + [fixed(w) for w in (cross_bias, cross_norm, bias_rows, self_norm)],
        out_specs=[row_spec, row_spec] + [triple_spec, probs_spec, pair_spec, row_spec, row_spec, scale_spec] * 2,
        out_shape=[row_bf16, row_bf16] + [triple_bf16, probs_bf16, pair_f32, row_bf16, row_f32, scale_f32] * 2,
        scratch_shapes=[
            scratch(size, width, kind=f32), scratch(size, width), stage, stage,
            scratch(steps, slots, TILE, width), *[scratch(items, LANES, kind=jnp.int32)] * 2,
            scratch(width, 3 * width), scratch(width, width), scratch(width, 3 * width), scratch(width, width),
            *semaphores(steps + 1), pltpu.SemaphoreType.DMA((4,)),
        ],
        compiler_params=remote(0),
        cost_estimate=cost(12, 40_000_000),
    )(lengths, slot_rows, slot_rows, cross_proj, cross_out, self_proj, self_out, cross_bias, cross_norm, bias_rows, self_norm)

    chunks = deep // width
    half, quarter = width // 2, width // 4
    total = 4 * width + LANES
    (output, grad_attended, up_sum, ffn_sum, down_kept, down_sent, up_kept, up_sent) = pl.pallas_call(
        functools.partial(
            ffn_kernel, slots, steps, digits[:chunk_bits], deep // places, z_digits, share, [(axis, bit, 1 << number) for number, (axis, bit, _) in enumerate(digits[chunk_bits:])]),
        grid=(steps + 1,),
        in_specs=[smem, smem, held(row_spec), held(item_spec), any_spec, any_spec]
        + [fixed(w) for w in (self_norm, up_bias, down_bias, ffn_norm)],
        out_specs=[held(item_spec), held(row_spec), total_of(1, deep), total_of(3, width)]
        + [kept_out(chunks * quarter, width)] * 2 + [kept_out(quarter, deep)] * 2,
        out_shape=[shape_of((slots, items, width), bf16), row_f32, shape_of((1, deep), f32), shape_of((3, width), f32)]
        + [shape_of((chunks * quarter, width), bf16)] * 2 + [shape_of((quarter, deep), bf16)] * 2,
        scratch_shapes=[
            scratch(width, deep), scratch(deep, width), scratch(rows, width), scratch(rows, deep), scratch(rows, width),
            scratch(rows, deep), scratch(size, deep, kind=f32), scratch(size, width, kind=f32), scratch(TILE, LANES, kind=jnp.int32),
            *[scratch(chunks, width, width), scratch(chunks, half, width)] * 2,
            pltpu.SemaphoreType.DMA((2,)), *semaphores(chunks), *semaphores(chunks),
        ],
        compiler_params=remote(1),
        cost_estimate=cost(36, 40_000_000),
    )(lengths, task_flags, normed2, slot_cotangent, ffn_up, ffn_down, self_norm, up_bias, down_bias, ffn_norm)

    grad_crossed, down_half, up_half, self_kept, self_sent = pl.pallas_call(
        functools.partial(self_kernel, slots, steps, digits, z_digits, share),
        grid=(steps + 1,),
        in_specs=[held(spec) for spec in (row_spec, row_spec, scale_spec, row_spec, triple_spec, probs_spec, pair_spec)]
        + [fixed(w) for w in (cross_norm, self_norm, ffn_sum, up_sum)] + [any_spec] * 7,
        out_specs=[held(row_spec), kept_out(chunks * quarter, width), kept_out(quarter, deep)] + [kept_out(quarter, total)] * 2,
        out_shape=[row_f32, shape_of((chunks * quarter, width), bf16), shape_of((quarter, deep), bf16)]
        + [shape_of((quarter, total), bf16)] * 2,
        scratch_shapes=[
            stage, out_stage, scratch(width, 3 * width), scratch(width, width), scratch(rows, width),
            scratch(rows, width), scratch(rows, width), scratch(rows, 3 * width), scratch(LANES, width, kind=f32),
            scratch(5, width, width), scratch(5, half, width),
            scratch(chunks * quarter, width), scratch(chunks * quarter, width), scratch(chunks * quarter // 2, width),
            scratch(quarter, deep), scratch(quarter, deep), scratch(quarter // 2, deep),
            pltpu.SemaphoreType.DMA((5,)), *semaphores(5), *semaphores(8),
        ],
        compiler_params=remote(2),
        cost_estimate=cost(18, 40_000_000),
    )(grad_attended, normed2, scale2, normed1, triple2, probs2, contexts2, cross_norm, self_norm, ffn_sum, up_sum,
      self_proj, self_out, context2, down_kept, down_sent, up_kept, up_sent)

    left = width // 16
    finish = bits == 4
    cross_left = left // 2 if finish else left
    box = 3 * width // 2
    rest_rows = chunks * quarter // 4
    tails = [(left, total), (cross_left, total)]
    grad_hidden, own_down, own_up, own_self, own_cross = pl.pallas_call(
        functools.partial(cross_kernel, slots, steps, cross_digits, cross_share, finish),
        grid=(steps + 1,),
        in_specs=[held(spec) for spec in (row_spec, row_spec, scale_spec, triple_spec, probs_spec, pair_spec)]
        + [fixed(cross_norm)] + [any_spec] * 9,
        out_specs=[any_spec, kept_out(rest_rows, width), kept_out(left, deep)] + [kept_out(*shape) for shape in tails],
        out_shape=[shape_of((slots, items, width), bf16), shape_of((rest_rows, width), f32), shape_of((left, deep), f32)]
        + [shape_of(shape, f32) for shape in tails],
        scratch_shapes=[
            stage, out_stage, scratch(width, 3 * width), scratch(width, width), scratch(2, rows, width),
            scratch(rows, width), scratch(rows, 3 * width), scratch(rows, width, kind=f32), scratch(LANES, width, kind=f32),
            scratch(steps, slots, TILE, width), scratch(steps, slots, TILE, width), scratch(5, width, width), scratch(5, half, width),
            scratch(width, width, kind=f32),
            scratch(2, 2, 2, left, total), scratch(3, 2, 2, left, box), scratch(3, 2, left, box), scratch(3, left, box),
            scratch(32, total), scratch(32, total),
            scratch(4 * rest_rows, width), scratch(2 * rest_rows, width), scratch(rest_rows, width),
            scratch(4 * left, deep), scratch(2 * left, deep), scratch(left, deep),
            scratch(quarter, total), scratch(quarter, total), scratch(quarter // 2, total), scratch(left, total),
            pltpu.SemaphoreType.DMA((8,)), *semaphores(5), *semaphores(steps), *semaphores(14), *semaphores(12),
            pltpu.SemaphoreType.DMA((steps,)),
        ],
        compiler_params=remote(3),
        cost_estimate=cost(18, 40_000_000),
    )(grad_crossed, normed1, scale1, triple1, probs1, contexts1, cross_norm, cross_proj, cross_out, dense, far_dense, context1,
      down_half, up_half, self_kept, self_sent)

    def sum_rest(total, first):
        for bit in range(first, bits):
            half = total.shape[0] // 2
            total = total[:half].astype(f32) + send(total[half:].astype(bf16), "dp", bit).astype(f32)
        return total

    own_down, own_up = sum_rest(own_down, 4), sum_rest(own_up, 4)
    own_self = sum_rest(own_self, 4)
    own_cross = sum_rest(own_cross, 4 if finish else 3)
    share, cross_share = own_self.shape[0], own_cross.shape[0]
    shapes = [
        (slots, items, width), (slots, items, width), own_down.shape, own_up.shape, (share, 3 * width), (share, width), (3, 1, share), (2, share),
        (1, share), (2, share), (1, deep // places), (cross_share, 3 * width), (cross_share, width), (3, cross_share), (2, cross_share),
    ]
    (output, grad_hidden, own_down, own_up, own_self_proj, own_self_out, self_vectors, self_norms, down_vector, ffn_norms, small_up,
     own_cross_proj, own_cross_out, cross_vectors, cross_norms) = pl.pallas_call(
        unpack_kernel,
        in_specs=[vmem_spec] * 6,
        out_specs=[vmem_spec] * len(shapes),
        out_shape=[shape_of(shape, bf16 if at < 2 else f32) for at, shape in enumerate(shapes)],
        compiler_params=params,
        cost_estimate=cost(0, 10_000_000),
    )(output, grad_hidden, own_down, own_up, own_self, own_cross)
    output, grad_hidden = (jnp.transpose(entry, (1, 0, 2))[None] for entry in (output, grad_hidden))
    return (
        output,
        grad_hidden,
        own_cross_proj,
        cross_vectors,
        cross_norms,
        own_cross_out,
        own_self_proj[None],
        jnp.transpose(self_vectors, (1, 0, 2)),
        self_norms[None],
        own_self_out[None],
        own_up[None],
        small_up,
        own_down[None],
        down_vector,
        ffn_norms[None],
    )


def solution(mesh):
    in_specs = (
        P("stream", "dp", None, None),
        P("stream", "dp"),
        P("stream", "dp"),
        P("stream", "dp", None, None),
        P(),
        P(),
        P(),
        P(),
        P("stream", None, None),
        P("stream", None, None),
        P("stream", None, None),
        P("stream", None, None),
        P("stream", None, None),
        P("stream", None),
        P("stream", None, None),
        P("stream", None),
        P("stream", None, None),
    )
    out_specs = (
        P("stream", "dp", None, None),
        P("stream", "dp", None, None),
        P(("stream", "dp"), None),
        P(None, ("stream", "dp")),
        P(None, ("stream", "dp")),
        P(("stream", "dp"), None),
        P("stream", "dp", None),
        P("stream", None, "dp"),
        P("stream", None, "dp"),
        P("stream", "dp", None),
        P("stream", "dp", None),
        P("stream", "dp"),
        P("stream", "dp", None),
        P("stream", "dp"),
        P("stream", None, "dp"),
    )
    return jax.shard_map(local, mesh=mesh, in_specs=in_specs, out_specs=out_specs, check_vma=False)
```
